128 devices in a mesh: freq: 8 (over x, core), tile: 16 (over y, z).
Axes of the slice: x: 4, y: 4, z: 4, core: 2. Of those that a mesh axis runs over, the one named last changes fastest.
Arguments:
- plus_time: bfloat16 [128, 128, 12288], P('freq', None, 'tile'), may hold values from -6 to 6
- minus_time: bfloat16 [128, 128, 12288], P('freq', None, 'tile'), may hold values from -6 to 6
- gate_starts: int32 [128, 48], P('freq', 'tile'), may hold values from 0 to 64
- tile_ranks: int32 [8, 48, 48], P('freq', None, 'tile'), may hold values from 1 to 64, as said below
- u_factors: bfloat16 [8, 48, 48, 2, 64, 256], P('freq', 'tile'), may hold values from -0.109375 to 0.109375
- v_factors: bfloat16 [8, 48, 48, 2, 64, 256], P('freq', None, 'tile'), may hold values from -0.375 to 0.375
Outputs:
- minus_new: bfloat16 [8, 2, 128, 12288], P('freq', None, None, 'tile')
- plus_new: bfloat16 [8, 2, 128, 12288], P('freq', None, None, 'tile')
- cross_gram: float32 [8, 2, 128, 128], P('freq', None, 'tile')
- normal_gram: float32 [8, 2, 128, 128], P('freq', None, 'tile')
The draws below stay inside these ranges and needn't reach their ends.
Inputs may be any that keep to these rules, and one draw needn't show every extreme that they name: `tile_ranks`: tiles with |i - j| <= 1 have rank 64; every other tile has rank at most 32, and some tile of every draw has exactly 32.
All inputs are finite; a program needn't handle non-finite values.
Results may differ from the reference program's by a relative error of at most 0.014.
Values may be sent and summed in bfloat16 or wider, within the bound.
No kernel may reach another device: no remote copies, remote signals or barrier semaphores. Data moves between devices by JAX's collectives and lax.ppermute only.
A program may use at most 192 MiB of HBM per device.

```python
import math
import jax
import jax.numpy as jnp
from jax import lax

S = 128
R = 12288
TILE = 256
KMAX = 64
GATE = 64
NSAMP = 128
NT = 48
F = 8


def draw_tile_ranks(key, part):
    base_ranks = jax.random.randint(jax.random.fold_in(key, 11), (F, NT, NT), KMAX // 4, KMAX // 2 + 1)
    row_ids = lax.broadcasted_iota(jnp.int32, (F, NT, NT), 1)
    col_ids = lax.broadcasted_iota(jnp.int32, (F, NT, NT), 2)
    near_diag = jnp.abs(row_ids - col_ids) <= 1
    corner = (row_ids == 0) & (col_ids == NT - 1)
    base_ranks = jnp.where(corner, KMAX // 2, base_ranks)
    return jnp.where(near_diag, KMAX, base_ranks).astype(jnp.int32)


def set_ends(result, key, smallest, largest):
    place = [jax.random.randint(jax.random.fold_in(key, axis), (), 0, length) for axis, length in enumerate(result.shape)]
    main_axis = result.shape.index(max(result.shape))
    neighbour = place[:main_axis] + [(place[main_axis] + 1) % result.shape[main_axis]] + place[main_axis + 1:]
    return result.at[tuple(place)].set(smallest).at[tuple(neighbour)].set(largest)


def block_scale(stream_key, shape, shards, low, high):
    gain, own = 1.0, jax.random.fold_in(stream_key, 6)
    for axis_at, shards_of in shards:
        draws = jnp.exp(jax.random.uniform(jax.random.fold_in(own, axis_at), (shards_of,), jnp.float32, low / len(shards), high / len(shards)))
        gain = gain * jnp.repeat(draws, shape[axis_at] // shards_of).reshape([-1 if axis == axis_at else 1 for axis in range(len(shape))])
    return gain


def scatter_about(rng, dims, width, bound, cuts=(), kind=jnp.bfloat16):
    level = block_scale(rng, dims, cuts, -0.22, 0.18) if cuts else 1.0
    values = jax.random.normal(rng, dims, jnp.float32) * width * level
    return jnp.minimum(jnp.maximum(values, -bound), bound).astype(kind)


def setup_inputs(seed: int = 0) -> dict:
    arg_keys = jax.random.split(jax.random.key(seed), 7)
    plus_time = scatter_about(arg_keys[0], (S, NSAMP, R), 1.0, 6.0, ((0, 8), (2, 16)))
    minus_time = scatter_about(arg_keys[1], (S, NSAMP, R), 1.0, 6.0, ((0, 8), (2, 16)))
    gate_starts = set_ends(jax.random.randint(arg_keys[2], (S, NT), 0, NSAMP - GATE + 1), jax.random.fold_in(arg_keys[2], 1), 0, NSAMP - GATE).astype(jnp.int32)
    tile_ranks = draw_tile_ranks(jax.random.fold_in(arg_keys[6], 71), 0)
    u_factors = scatter_about(arg_keys[4], (F, NT, NT, 2, KMAX, TILE), (NT * KMAX) ** -0.5, 0.109375, ((0, 8), (1, 16)))
    v_factors = scatter_about(arg_keys[5], (F, NT, NT, 2, KMAX, TILE), TILE ** -0.5, 0.375, ((0, 8), (2, 16)))
    return dict(plus_time=plus_time, minus_time=minus_time, gate_starts=gate_starts, tile_ranks=tile_ranks, u_factors=u_factors, v_factors=v_factors)


def make_table(freq_count, sample_count):
    freq_ids = lax.broadcasted_iota(jnp.int32, (freq_count, sample_count), 0)
    sample_ids = lax.broadcasted_iota(jnp.int32, (freq_count, sample_count), 1)
    phase_ids = freq_ids * sample_ids % sample_count
    angles = phase_ids.astype(jnp.float32) * (2.0 * math.pi / sample_count)
    amplitude = 1.0 / math.sqrt(GATE)
    return jnp.stack([jnp.cos(angles) * amplitude, -jnp.sin(angles) * amplitude]).astype(jnp.bfloat16)

def half_signs(entry_count):
    entry_ids = lax.broadcasted_iota(jnp.int32, (entry_count,), 0)
    return jnp.where(entry_ids < entry_count // 2, 1.0, -1.0).astype(jnp.float32)

def reference(plus_time, minus_time, gate_starts, tile_ranks, u_factors, v_factors):
    tile_count = R // TILE
    dft_table = make_table(F, NSAMP)
    flat_table = dft_table.reshape(2 * F, NSAMP)

    def one_source(src_items):
        plus_row, minus_row, gate_row = src_items
        starts = jnp.repeat(gate_row, TILE)[None, :]
        sample_ids = jnp.arange(NSAMP, dtype=jnp.int32)[:, None]
        inside = (sample_ids >= starts) & (sample_ids < starts + GATE)
        zero_val = jnp.zeros((), plus_row.dtype)
        plus_spec = jnp.dot(flat_table, jnp.where(inside, plus_row, zero_val), preferred_element_type=jnp.float32)
        minus_spec = jnp.dot(flat_table, jnp.where(inside, minus_row, zero_val), preferred_element_type=jnp.float32)
        return jnp.stack([plus_spec, minus_spec]).reshape(2, 2, F, R)
    per_source = lax.map(one_source, (plus_time, minus_time, gate_starts))
    spectra = jnp.transpose(per_source, (3, 2, 1, 0, 4)).astype(jnp.bfloat16)
    sign_vec = half_signs(2 * S)
    rank_ids = jnp.arange(KMAX, dtype=jnp.int32)

    def one_freq(freq_items):
        spec_freq, u_freq, v_freq, rank_freq = freq_items
        columns = spec_freq.reshape(2, 2 * S, tile_count, TILE).astype(jnp.float32)

        def one_row(row_items):
            u_row, v_row, ranks_row = row_items
            partial_c = jnp.einsum('jckr,dsjr->jcdks', v_row.astype(jnp.float32), columns, precision=lax.Precision.HIGHEST)
            coeff_real = partial_c[:, 0, 0] - sign_vec * partial_c[:, 1, 1]
            coeff_imag = partial_c[:, 0, 1] + sign_vec * partial_c[:, 1, 0]
            rank_mask = (rank_ids[None, :] < ranks_row[:, None]).astype(jnp.float32)[:, :, None]
            coeff_all = jnp.stack([coeff_real * rank_mask, coeff_imag * rank_mask], 1).astype(jnp.bfloat16)
            products = jnp.einsum('jckr,jeks->cesr', u_row.astype(jnp.float32), coeff_all.astype(jnp.float32), precision=lax.Precision.HIGHEST)
            resp_real = products[0, 0] - sign_vec[:, None] * products[1, 1]
            resp_imag = products[0, 1] + sign_vec[:, None] * products[1, 0]
            return jnp.stack([resp_real, resp_imag])
        rows_out = lax.map(one_row, (u_freq, v_freq, rank_freq))
        return jnp.transpose(rows_out, (1, 2, 0, 3)).reshape(2, 2 * S, R)
    response = lax.map(one_freq, (spectra, u_factors, v_factors, tile_ranks))
    rounded = response.astype(jnp.bfloat16)
    minus_new = rounded[:, :, :S]
    plus_new = rounded[:, :, S:]
    gram_parts = jnp.einsum('fczr,fesr->fczes', rounded.astype(jnp.float32), plus_new.astype(jnp.float32), precision=lax.Precision.HIGHEST)
    gram_real = gram_parts[:, 0, :, 0] + gram_parts[:, 1, :, 1]
    gram_imag = gram_parts[:, 1, :, 0] - gram_parts[:, 0, :, 1]
    cross_gram = jnp.stack([gram_real[:, :S], gram_imag[:, :S]], 1) / math.sqrt(R)
    normal_gram = jnp.stack([gram_real[:, S:], gram_imag[:, S:]], 1) / R
    return (minus_new, plus_new, cross_gram, normal_gram)
```

```python
import functools
import math

import jax
import jax.numpy as jnp
from jax import lax
from jax.experimental import pallas as pl
from jax.experimental.pallas import tpu as pltpu
from jax.sharding import Mesh
from jax.sharding import PartitionSpec as P

R = 12288
GATE = 64
TILE = 256
HALF = 32
FREQ = ("fx", "fc")
TILES = ("ty", "tz")
BF = jnp.bfloat16
F32 = jnp.float32


def make_table(freq_count, sample_count):
    freq_ids = lax.broadcasted_iota(jnp.int32, (freq_count, sample_count), 0)
    sample_ids = lax.broadcasted_iota(jnp.int32, (freq_count, sample_count), 1)
    phase_ids = freq_ids * sample_ids % sample_count
    angles = phase_ids.astype(F32) * (2.0 * math.pi / sample_count)
    amplitude = 1.0 / math.sqrt(GATE)
    return jnp.stack([jnp.cos(angles) * amplitude, -jnp.sin(angles) * amplitude]).astype(BF)


def params(mib=56):
    return pltpu.CompilerParams(vmem_limit_bytes=mib * 2**20)


def dft_kernel(starts_ref, tab_ref, plus_ref, minus_ref, out_ref):
    b = pl.program_id(0)
    lane = lax.broadcasted_iota(jnp.int32, (1, 256), 1)
    sample = lane & 127
    upper = lane >= 128
    row_source = lax.broadcasted_iota(jnp.int32, (256, 256), 0) & 15
    acc = [jnp.zeros((256, 256), F32), jnp.zeros((256, 256), F32)]
    for p in range(8):
        start = jnp.where(upper, starts_ref[2 * p + 1, b], starts_ref[2 * p, b])
        inside = (sample >= start) & (sample < start + GATE)
        source = jnp.where(inside, jnp.where(upper, 2 * p + 1, 2 * p), -1)
        table = jnp.where(row_source == source, tab_ref[...], 0.0).astype(BF)
        for q, ref in enumerate((plus_ref, minus_ref)):
            data = ref[2 * p : 2 * p + 2].reshape(256, 256)
            acc[q] += jnp.dot(table, data, preferred_element_type=F32)
    first = acc[0].reshape(8, 2, 16, 256)
    second = acc[1].reshape(8, 2, 16, 256)
    out_ref[:, 0, 0] = first[:, 0].astype(BF)
    out_ref[:, 1, 0] = first[:, 1].astype(BF)
    out_ref[:, 0, 1] = second[:, 0].astype(BF)
    out_ref[:, 1, 1] = (-second[:, 1]).astype(BF)


def dft(plus_time, minus_time, gate_starts, table):
    sources, samples, receivers = plus_time.shape
    blocks = receivers // TILE
    data = pl.BlockSpec((sources, samples, TILE), lambda b: (0, 0, b))
    return pl.pallas_call(
        dft_kernel,
        grid=(blocks,),
        in_specs=[
            pl.BlockSpec(memory_space=pltpu.SMEM),
            pl.BlockSpec((256, 256), lambda b: (0, 0)),
            data,
            data,
        ],
        out_specs=pl.BlockSpec((8, 2, 2, 16, TILE), lambda b: (0, 0, 0, 0, b)),
        out_shape=jax.ShapeDtypeStruct((8, 2, 2, 16, receivers), BF),
        compiler_params=params(),
        cost_estimate=pl.CostEstimate(
            flops=2 * 2 * 256 * 2048 * receivers, bytes_accessed=7 * 2**20, transcendentals=0
        ),
    )(gate_starts, table, plus_time, minus_time)


def fill_weights(w_ref, x_ref):
    for q in range(2):
        re = x_ref[:, 0, q].reshape(128, TILE).T
        im = x_ref[:, 1, q].reshape(128, TILE).T
        near, far = slice(q * 128, (q + 1) * 128), slice(256 + q * 128, 384 + q * 128)
        w_ref[0:256, near] = re
        w_ref[0:256, far] = im
        w_ref[256:512, near] = -im
        w_ref[256:512, far] = re


def coeff_kernel(ichunk, ranks_ref, x_ref, v_ref, out_ref, w_ref):
    j, ic = pl.program_id(0), pl.program_id(1)

    @pl.when(ic == 0)
    def _():
        fill_weights(w_ref, x_ref)

    prod = jnp.dot(
        v_ref[:, 0, 0].reshape(ichunk * HALF, TILE), w_ref[0:256], preferred_element_type=F32
    )
    prod += jnp.dot(
        v_ref[:, 0, 1].reshape(ichunk * HALF, TILE), w_ref[256:512], preferred_element_type=F32
    )
    rank_ids = lax.broadcasted_iota(jnp.int32, (HALF, 512), 0)
    for ii in range(ichunk):
        tile = prod[ii * HALF : (ii + 1) * HALF]
        kept = jnp.where(rank_ids < ranks_ref[ic * ichunk + ii, j], tile, 0.0)
        out_ref[ii // 3, ii % 3, 0] = kept.astype(BF)


def coefficients(spectra, v_factors, ranks):
    rows, cols = v_factors.shape[:2]
    ichunk = rows // 2
    return pl.pallas_call(
        functools.partial(coeff_kernel, ichunk),
        grid=(cols, rows // ichunk),
        in_specs=[
            pl.BlockSpec(memory_space=pltpu.SMEM),
            pl.BlockSpec((8, 2, 2, 16, TILE), lambda j, i: (0, 0, 0, 0, j)),
            pl.BlockSpec((ichunk, 1, 2, HALF, TILE), lambda j, i: (i, j, 0, 0, 0)),
        ],
        out_specs=pl.BlockSpec((ichunk // 3, 3, 1, HALF, 512), lambda j, i: (i, 0, j, 0, 0)),
        out_shape=jax.ShapeDtypeStruct((rows // 3, 3, cols, HALF, 512), BF),
        scratch_shapes=[pltpu.VMEM((512, 512), BF)],
        compiler_params=params(),
        cost_estimate=pl.CostEstimate(
            flops=2 * rows * cols * HALF * 512 * 512, bytes_accessed=10 * 2**20, transcendentals=0
        ),
    )(ranks, spectra, v_factors)


def band_kernel(place_ref, ranks_ref, x_ref, va_ref, vb_ref, vc_ref, band_ref, up_ref, down_ref, w_ref):
    jl = pl.program_id(0)
    last_row = ranks_ref.shape[0] - 1
    fill_weights(w_ref, x_ref)
    refs = (va_ref, vb_ref, vc_ref)
    prod = jnp.dot(
        jnp.concatenate([ref[0, 0, 0] for ref in refs], axis=0),
        w_ref[0:256],
        preferred_element_type=F32,
    )
    prod += jnp.dot(
        jnp.concatenate([ref[0, 0, 1] for ref in refs], axis=0),
        w_ref[256:512],
        preferred_element_type=F32,
    )
    rank_ids = lax.broadcasted_iota(jnp.int32, (HALF, 512), 0) + HALF
    kept = []
    for n in range(3):
        i = place_ref[0] * 3 + jl + n - 1
        rank = ranks_ref[jnp.clip(i, 0, last_row), jl]
        rank = jnp.where((i >= 0) & (i <= last_row), rank, 0)
        kept.append(jnp.where(rank_ids < rank, prod[n * HALF : (n + 1) * HALF], 0.0).astype(BF))

    @pl.when(jl == 0)
    def _():
        band_ref[...] = jnp.zeros_like(band_ref)
        up_ref[...] = kept[0]

    @pl.when(jl == 2)
    def _():
        down_ref[...] = kept[2]

    for n in range(3):
        il = jl + n - 1

        @pl.when((il >= 0) & (il < 3))
        def _():
            band_ref[il, 2 - n] = kept[n]


def band_coefficients(spectra, v_factors, ranks, place):
    rows = v_factors.shape[0]

    def spec(off):
        return pl.BlockSpec(
            (1, 1, 2, HALF, TILE),
            lambda j, place: (jnp.clip(place[0] * 3 + j + off, 0, rows - 1), j, 0, 1, 0),
        )

    edge = pl.BlockSpec((HALF, 512), lambda j, place: (0, 0))
    return pl.pallas_call(
        band_kernel,
        grid_spec=pltpu.PrefetchScalarGridSpec(
            num_scalar_prefetch=1,
            grid=(3,),
            in_specs=[
                pl.BlockSpec(memory_space=pltpu.SMEM),
                pl.BlockSpec((8, 2, 2, 16, TILE), lambda j, place: (0, 0, 0, 0, j)),
                spec(-1),
                spec(0),
                spec(1),
            ],
            out_specs=[
                pl.BlockSpec((3, 4, HALF, 512), lambda j, place: (0, 0, 0, 0)),
                edge,
                edge,
            ],
            scratch_shapes=[pltpu.VMEM((512, 512), BF)],
        ),
        out_shape=[
            jax.ShapeDtypeStruct((3, 4, HALF, 512), BF),
            jax.ShapeDtypeStruct((HALF, 512), BF),
            jax.ShapeDtypeStruct((HALF, 512), BF),
        ],
        compiler_params=params(),
        cost_estimate=pl.CostEstimate(
            flops=2 * 9 * HALF * 512 * 512, bytes_accessed=2 * 2**20, transcendentals=0
        ),
    )(place, ranks, spectra, v_factors, v_factors, v_factors)


def turn_kernel(chunks, place_ref, u_ref, ua_ref, ub_ref, uc_ref, low_ref, band_ref):
    g = pl.program_id(1)
    for c in range(2):
        for n in range(chunks):
            part = u_ref[0, n * 8 : (n + 1) * 8, c].reshape(256, TILE)
            low_ref[0, c, :, n * 256 : (n + 1) * 256] = part.T

    @pl.when(g == 0)
    def _():
        for c in range(2):
            parts = [r[0, 0, c] for r in (ua_ref, ub_ref, uc_ref)]
            part = jnp.concatenate([*parts, jnp.zeros_like(parts[0])], axis=0)
            band_ref[0, c] = part.T


def turned(u_factors, place):
    rows, all_cols = u_factors.shape[:2]

    def spec(off):
        return pl.BlockSpec(
            (1, 1, 2, HALF, TILE),
            lambda i, g, place: (i, jnp.clip(place[0] * 3 + i + off, 0, all_cols - 1), 0, 1, 0),
        )

    return pl.pallas_call(
        functools.partial(turn_kernel, 3),
        grid_spec=pltpu.PrefetchScalarGridSpec(
            num_scalar_prefetch=1,
            grid=(rows, 2),
            in_specs=[
                pl.BlockSpec((1, all_cols // 2, 2, HALF, TILE), lambda i, g, place: (i, g, 0, 0, 0)),
                spec(-1),
                spec(0),
                spec(1),
            ],
            out_specs=[
                pl.BlockSpec((1, 2, TILE, all_cols * HALF // 2), lambda i, g, place: (i, 0, 0, g)),
                pl.BlockSpec((1, 2, TILE, 128), lambda i, g, place: (i, 0, 0, 0)),
            ],
        ),
        out_shape=[
            jax.ShapeDtypeStruct((rows, 2, TILE, all_cols * HALF), BF),
            jax.ShapeDtypeStruct((rows, 2, TILE, 128), BF),
        ],
        compiler_params=params(),
        cost_estimate=pl.CostEstimate(flops=10**9, bytes_accessed=10 * 2**20, transcendentals=0),
    )(place, u_factors, u_factors, u_factors, u_factors)


def across(a, b):
    return lax.dot_general(a, b, (((1,), (1,)), ((), ())), preferred_element_type=F32)


def response_kernel(
    groups, c_ref, u_ref, band_ref, up_ref, down_ref, ub_ref,
    minus_ref, plus_ref, gram_ref, acc, gram_acc,
):
    i, g = pl.program_id(0), pl.program_id(1)
    sources, _, cols = c_ref.shape[:3]
    depth = sources * cols * HALF
    left = u_ref[0].reshape(512, depth)
    prod = jnp.dot(left, c_ref[:, 0].reshape(depth, 512), preferred_element_type=F32)

    @pl.when(g == 0)
    def _():
        acc[...] = prod

    @pl.when(g > 0)
    def _():
        acc[...] += prod

    @pl.when(g == groups - 1)
    def _():
        first = jnp.where(i == 0, up_ref[...], band_ref[0, 0])
        last = jnp.where(i == 2, down_ref[...], band_ref[0, 2])
        upper = jnp.concatenate([first, band_ref[0, 1], last, band_ref[0, 3]], axis=0)
        total = acc[...] + jnp.dot(ub_ref[0].reshape(512, 128), upper, preferred_element_type=F32)
        re = total[:256, :256] - total[256:, 256:]
        im = total[256:, :256] + total[:256, 256:]
        z_re = re.T.astype(BF)
        im = im.T
        z_im = jnp.concatenate([im[:128], -im[128:]], axis=0).astype(BF)
        p_re, p_im = z_re[128:], z_im[128:]
        minus_ref[0, 0] = z_re[:128]
        minus_ref[0, 1] = z_im[:128]
        plus_ref[0, 0] = p_re
        plus_ref[0, 1] = p_im
        g_re = across(z_re, p_re) + across(z_im, p_im)
        g_im = across(z_im, p_re) - across(z_re, p_im)

        @pl.when(i == 0)
        def _():
            gram_acc[0] = g_re
            gram_acc[1] = g_im

        @pl.when(i > 0)
        def _():
            gram_acc[0] += g_re
            gram_acc[1] += g_im

        @pl.when(i == 2)
        def _():
            for m, scale in enumerate((1.0 / math.sqrt(R), 1.0 / R)):
                for c in range(2):
                    part = gram_acc[c, m * 128 : (m + 1) * 128] * scale
                    gram_ref[:, m, c] = part.reshape(16, 8, 128)


def respond(coeffs, turned_low, turned_band, band, up, down):
    sources = coeffs.shape[0]
    rows = turned_low.shape[0]
    groups = 2
    per = sources // groups
    edge = pl.BlockSpec((HALF, 512), lambda i, g: (0, 0))
    field = pl.BlockSpec((1, 2, 128, TILE), lambda i, g: (0, 0, 0, i))
    return pl.pallas_call(
        functools.partial(response_kernel, groups),
        grid=(rows, groups),
        in_specs=[
            pl.BlockSpec((per, 1, 3, HALF, 512), lambda i, g: (g, i, 0, 0, 0)),
            pl.BlockSpec((1, 2, TILE, 3 * per * HALF), lambda i, g: (i, 0, 0, g)),
            pl.BlockSpec((1, 4, HALF, 512), lambda i, g: (i, 0, 0, 0)),
            edge,
            edge,
            pl.BlockSpec((1, 2, TILE, 128), lambda i, g: (i, 0, 0, 0)),
        ],
        out_specs=[
            field,
            field,
            pl.BlockSpec((16, 2, 2, 8, 128), lambda i, g: (0, 0, 0, 0, 0)),
        ],
        scratch_shapes=[pltpu.VMEM((512, 512), F32), pltpu.VMEM((2, 256, 128), F32)],
        out_shape=[
            jax.ShapeDtypeStruct((1, 2, 128, rows * TILE), BF),
            jax.ShapeDtypeStruct((1, 2, 128, rows * TILE), BF),
            jax.ShapeDtypeStruct((16, 2, 2, 8, 128), F32),
        ],
        compiler_params=params(),
        cost_estimate=pl.CostEstimate(
            flops=2 * 144 * HALF * 512 * 512, bytes_accessed=11 * 2**20, transcendentals=0
        ),
    )(coeffs, turned_low, band, up, down, turned_band)


def on_device(plus_time, minus_time, gate_starts, tile_ranks, u_factors, v_factors):
    u_factors, v_factors, ranks = u_factors[0], v_factors[0], tile_ranks[0]
    place = lax.axis_index(TILES).astype(jnp.int32).reshape(1)
    rows = make_table(8, 128).astype(F32).transpose(1, 0, 2)
    rows = jnp.broadcast_to(rows[:, :, None], (8, 2, 16, 128)).reshape(256, 128)
    table = jnp.concatenate([rows, rows], axis=1)
    local_spec = dft(plus_time, minus_time, gate_starts, table)
    spectra = lax.all_to_all(local_spec, FREQ, 0, 0, tiled=True)
    band, up, down = band_coefficients(spectra, v_factors, ranks, place)
    size = lax.axis_size(TILES)
    from_below = lax.ppermute(down, TILES, [(i, i + 1) for i in range(size - 1)])
    from_above = lax.ppermute(up, TILES, [(i + 1, i) for i in range(size - 1)])
    spectra, band = lax.optimization_barrier((spectra, band))
    coeffs = coefficients(spectra, v_factors, ranks)
    coeffs, from_below, from_above = lax.optimization_barrier((coeffs, from_below, from_above))
    arrived = lax.all_to_all(coeffs, TILES, 0, 0, tiled=True)
    low, low_band = turned(u_factors, place)
    minus_new, plus_new, gram = respond(arrived, low, low_band, band, from_below, from_above)
    sums = lax.all_to_all(gram, TILES, 0, 0, tiled=True).sum(axis=0)
    return (minus_new, plus_new, sums[None, 0], sums[None, 1])


def solution(mesh):
    torus = Mesh(mesh.devices.reshape(4, 2, 4, 4), (*FREQ, *TILES))
    in_specs = (
        P(FREQ, None, TILES),
        P(FREQ, None, TILES),
        P(FREQ, TILES),
        P(FREQ, None, TILES),
        P(FREQ, TILES, None, None, None, None),
        P(FREQ, None, TILES, None, None, None),
    )
    out_specs = (
        P(FREQ, None, None, TILES),
        P(FREQ, None, None, TILES),
        P(FREQ, None, TILES, None),
        P(FREQ, None, TILES, None),
    )
    return jax.shard_map(
        on_device, mesh=torus, in_specs=in_specs, out_specs=out_specs, check_vma=False
    )
```

```python
import functools
import math

import jax
import jax.numpy as jnp
from jax import lax
from jax.experimental import pallas as pl
from jax.experimental.pallas import tpu as pltpu
from jax.sharding import Mesh
from jax.sharding import PartitionSpec as P

R = 12288
GATE = 64
TILE = 256
HALF = 32
FREQ = ("fx", "fc")
TILES = ("ty", "tz")
BF = jnp.bfloat16
F32 = jnp.float32


def make_table(freq_count, sample_count):
    freq_ids = lax.broadcasted_iota(jnp.int32, (freq_count, sample_count), 0)
    sample_ids = lax.broadcasted_iota(jnp.int32, (freq_count, sample_count), 1)
    phase_ids = freq_ids * sample_ids % sample_count
    angles = phase_ids.astype(F32) * (2.0 * math.pi / sample_count)
    amplitude = 1.0 / math.sqrt(GATE)
    return jnp.stack([jnp.cos(angles) * amplitude, -jnp.sin(angles) * amplitude]).astype(BF)


def params(mib=56):
    return pltpu.CompilerParams(vmem_limit_bytes=mib * 2**20)


def dft_kernel(starts_ref, tab_ref, plus_hbm, minus_hbm, out_ref, t_ref, data_ref, sems):
    copies = []
    for b in range(3):
        for q, ref in enumerate((plus_hbm, minus_hbm)):
            src = ref.at[:, :, pl.ds(b * TILE, TILE)]
            copies.append(pltpu.make_async_copy(src, data_ref.at[b, q], sems.at[b, q]))
            copies[-1].start()
    lane = lax.broadcasted_iota(jnp.int32, (1, 256), 1)
    sample = lane & 127
    upper = lane >= 128
    row_source = lax.broadcasted_iota(jnp.int32, (256, 256), 0) & 15
    for b in range(3):
        for p in range(8):
            start = jnp.where(upper, starts_ref[b, 2 * p + 1], starts_ref[b, 2 * p])
            inside = (sample >= start) & (sample < start + GATE)
            source = jnp.where(inside, jnp.where(upper, 2 * p + 1, 2 * p), -1)
            table = jnp.where(row_source == source, tab_ref[...], 0.0).astype(BF)
            t_ref[b % 2, :, p * 256 : (p + 1) * 256] = table
        for q in range(2):
            copies[2 * b + q].wait()
            data = data_ref[b, q].reshape(2048, 256)
            prod = jnp.dot(t_ref[b % 2], data, preferred_element_type=F32)
            prod = prod.reshape(8, 2, 16, 256)
            lanes = slice(b * TILE, (b + 1) * TILE)
            out_ref[:, 0, q, :, lanes] = prod[:, 0].astype(BF)
            out_ref[:, 1, q, :, lanes] = (prod[:, 1] if q == 0 else -prod[:, 1]).astype(BF)


def dft(plus_time, minus_time, gate_starts, table):
    sources, samples, receivers = plus_time.shape
    return pl.pallas_call(
        dft_kernel,
        in_specs=[
            pl.BlockSpec(memory_space=pltpu.SMEM),
            pl.BlockSpec(memory_space=pltpu.VMEM),
            pl.BlockSpec(memory_space=pl.ANY),
            pl.BlockSpec(memory_space=pl.ANY),
        ],
        out_specs=pl.BlockSpec(memory_space=pltpu.VMEM),
        out_shape=jax.ShapeDtypeStruct((8, 2, 2, 16, receivers), BF),
        scratch_shapes=[
            pltpu.VMEM((2, 256, 2048), BF),
            pltpu.VMEM((3, 2, sources, samples, TILE), BF),
            pltpu.SemaphoreType.DMA((3, 2)),
        ],
        compiler_params=params(),
        cost_estimate=pl.CostEstimate(
            flops=2 * 2 * 256 * 2048 * receivers, bytes_accessed=7 * 2**20, transcendentals=0
        ),
    )(gate_starts, table, plus_time, minus_time)


def fill_weights(w_ref, x_ref):
    for q in range(2):
        re = x_ref[:, 0, q].reshape(128, TILE).T
        im = x_ref[:, 1, q].reshape(128, TILE).T
        near, far = slice(q * 128, (q + 1) * 128), slice(256 + q * 128, 384 + q * 128)
        w_ref[0:256, near] = re
        w_ref[0:256, far] = im
        w_ref[256:512, near] = -im
        w_ref[256:512, far] = re


def coeff_kernel(ranks_ref, x_ref, v_hbm, out_hbm, v_ref, o_ref, w_ref, sems):
    arrivals, sends = [], []
    for j in range(3):
        src = v_hbm.at[:, j, :, pl.ds(0, HALF), :]
        arrivals.append(pltpu.make_async_copy(src, v_ref.at[j], sems.at[0, j]))
        arrivals[-1].start()
    rank_ids = lax.broadcasted_iota(jnp.int32, (HALF, 512), 0)
    for j in range(3):
        fill_weights(w_ref, x_ref.at[:, :, :, :, pl.ds(j * TILE, TILE)])
        arrivals[j].wait()
        for h in range(4):
            rows = slice(h * 12, (h + 1) * 12)
            v = jnp.concatenate([v_ref[j, rows, c].reshape(12 * HALF, TILE) for c in range(2)], axis=1)
            prod = jnp.dot(v, w_ref[...], preferred_element_type=F32)
            for n in range(12):
                i = h * 12 + n
                kept = jnp.where(rank_ids < ranks_ref[j, i], prod[n * HALF : (n + 1) * HALF], 0.0)
                o_ref[j, i // 3, i % 3] = kept.astype(BF)
        sends.append(pltpu.make_async_copy(o_ref.at[j], out_hbm.at[:, :, j], sems.at[1, j]))
        sends[-1].start()
    for send in sends:
        send.wait()


def coefficients(spectra, v_factors, ranks):
    rows, cols = v_factors.shape[:2]
    return pl.pallas_call(
        coeff_kernel,
        in_specs=[
            pl.BlockSpec(memory_space=pltpu.SMEM),
            pl.BlockSpec(memory_space=pltpu.VMEM),
            pl.BlockSpec(memory_space=pl.ANY),
        ],
        out_specs=pl.BlockSpec(memory_space=pl.ANY),
        out_shape=jax.ShapeDtypeStruct((rows // 3, 3, cols, HALF, 512), BF),
        scratch_shapes=[
            pltpu.VMEM((cols, rows, 2, HALF, TILE), BF),
            pltpu.VMEM((cols, rows // 3, 3, HALF, 512), BF),
            pltpu.VMEM((512, 512), BF),
            pltpu.SemaphoreType.DMA((2, 3)),
        ],
        compiler_params=params(),
        cost_estimate=pl.CostEstimate(
            flops=2 * rows * cols * HALF * 512 * 512, bytes_accessed=10 * 2**20, transcendentals=0
        ),
    )(ranks, spectra, v_factors)


def band_kernel(place_ref, ranks_ref, x_ref, va_ref, vb_ref, vc_ref, band_ref, up_ref, down_ref, w_ref):
    jl = pl.program_id(0)
    last_row = ranks_ref.shape[1] - 1
    fill_weights(w_ref, x_ref)
    refs = (va_ref, vb_ref, vc_ref)
    prod = jnp.dot(
        jnp.concatenate([ref[0, 0, 0] for ref in refs], axis=0),
        w_ref[0:256],
        preferred_element_type=F32,
    )
    prod += jnp.dot(
        jnp.concatenate([ref[0, 0, 1] for ref in refs], axis=0),
        w_ref[256:512],
        preferred_element_type=F32,
    )
    rank_ids = lax.broadcasted_iota(jnp.int32, (HALF, 512), 0) + HALF
    kept = []
    for n in range(3):
        i = place_ref[0] * 3 + jl + n - 1
        rank = ranks_ref[jl, jnp.clip(i, 0, last_row)]
        rank = jnp.where((i >= 0) & (i <= last_row), rank, 0)
        kept.append(jnp.where(rank_ids < rank, prod[n * HALF : (n + 1) * HALF], 0.0).astype(BF))

    @pl.when(jl == 0)
    def _():
        band_ref[...] = jnp.zeros_like(band_ref)
        up_ref[...] = kept[0]

    @pl.when(jl == 2)
    def _():
        down_ref[...] = kept[2]

    for n in range(3):
        il = jl + n - 1

        @pl.when((il >= 0) & (il < 3))
        def _():
            band_ref[il, 2 - n] = kept[n]


def band_coefficients(spectra, v_factors, ranks, place):
    rows = v_factors.shape[0]

    def spec(off):
        return pl.BlockSpec(
            (1, 1, 2, HALF, TILE),
            lambda j, place: (jnp.clip(place[0] * 3 + j + off, 0, rows - 1), j, 0, 1, 0),
        )

    edge = pl.BlockSpec((HALF, 512), lambda j, place: (0, 0))
    return pl.pallas_call(
        band_kernel,
        grid_spec=pltpu.PrefetchScalarGridSpec(
            num_scalar_prefetch=1,
            grid=(3,),
            in_specs=[
                pl.BlockSpec(memory_space=pltpu.SMEM),
                pl.BlockSpec((8, 2, 2, 16, TILE), lambda j, place: (0, 0, 0, 0, j)),
                spec(-1),
                spec(0),
                spec(1),
            ],
            out_specs=[
                pl.BlockSpec((3, 3, HALF, 512), lambda j, place: (0, 0, 0, 0)),
                edge,
                edge,
            ],
            scratch_shapes=[pltpu.VMEM((512, 512), BF)],
        ),
        out_shape=[
            jax.ShapeDtypeStruct((3, 3, HALF, 512), BF),
            jax.ShapeDtypeStruct((HALF, 512), BF),
            jax.ShapeDtypeStruct((HALF, 512), BF),
        ],
        compiler_params=params(),
        cost_estimate=pl.CostEstimate(
            flops=2 * 9 * HALF * 512 * 512, bytes_accessed=2 * 2**20, transcendentals=0
        ),
    )(place, ranks, spectra, v_factors, v_factors, v_factors)


def response_kernel(
    place_ref, c_hbm, u_hbm, band_ref, up_ref, down_ref, minus_ref, plus_ref, gram_ref,
    c_ref, u_ref, b_ref, acc, sems,
):
    all_cols = u_hbm.shape[1]
    arrivals = []
    for i in range(3):
        low = pl.ds(0, HALF)
        pairs = [(c_hbm.at[:, i], c_ref.at[i]), (u_hbm.at[i, :, :, low, :], u_ref.at[i])]
        for n in range(3):
            col = jnp.clip(place_ref[0] * 3 + i + n - 1, 0, all_cols - 1)
            pairs.append((u_hbm.at[i, col, :, pl.ds(HALF, HALF), :], b_ref.at[i, n]))
        arrivals.append(
            [pltpu.make_async_copy(s, d, sems.at[i, k]) for k, (s, d) in enumerate(pairs)]
        )
        for copy in arrivals[-1]:
            copy.start()

    def product(c, u):
        right = jnp.concatenate(u, axis=1)
        return lax.dot_general(c, right, (((0,), (0,)), ((), ())), preferred_element_type=F32)

    for i in range(3):
        for copy in arrivals[i]:
            copy.wait()
        upper = [band_ref[i, n] for n in range(3)]
        if i == 0:
            upper[0] = up_ref[...]
        if i == 2:
            upper[2] = down_ref[...]
        prod = product(
            jnp.concatenate(upper, axis=0), [b_ref[i, :, c].reshape(3 * HALF, TILE) for c in range(2)]
        )
        prod += product(
            c_ref[i].reshape(all_cols * HALF, 512),
            [u_ref[i, :, c].reshape(all_cols * HALF, TILE) for c in range(2)],
        )
        re = (prod[:256, :256] - prod[256:, 256:]).astype(BF)
        im = prod[256:, :256] + prod[:256, 256:]
        im = jnp.concatenate([im[:128], -im[128:]], axis=0).astype(BF)
        lanes = slice(i * TILE, (i + 1) * TILE)
        minus_ref[0, 0, :, lanes] = re[:128]
        minus_ref[0, 1, :, lanes] = im[:128]
        plus_ref[0, 0, :, lanes] = re[128:]
        plus_ref[0, 1, :, lanes] = im[128:]
        gram = lax.dot_general(
            jnp.concatenate([re, im], axis=0),
            jnp.concatenate([re[128:], im[128:]], axis=0),
            (((1,), (1,)), ((), ())),
            preferred_element_type=F32,
        )
        if i == 0:
            acc[...] = gram
        else:
            acc[...] += gram
    gram = acc[...]
    parts = (gram[:256, :128] + gram[256:, 128:], gram[256:, :128] - gram[:256, 128:])
    for m, scale in enumerate((1.0 / math.sqrt(R), 1.0 / R)):
        for c, part in enumerate(parts):
            gram_ref[:, m, c] = (part[m * 128 : (m + 1) * 128] * scale).reshape(16, 8, 128)


def respond(coeffs, u_factors, band, up, down, place):
    rows, all_cols = u_factors.shape[:2]
    whole = pl.BlockSpec(memory_space=pltpu.VMEM)
    return pl.pallas_call(
        response_kernel,
        in_specs=[
            pl.BlockSpec(memory_space=pltpu.SMEM),
            pl.BlockSpec(memory_space=pl.ANY),
            pl.BlockSpec(memory_space=pl.ANY),
            whole,
            whole,
            whole,
        ],
        out_specs=[whole, whole, whole],
        scratch_shapes=[
            pltpu.VMEM((rows, all_cols // 3, 3, HALF, 512), BF),
            pltpu.VMEM((rows, all_cols, 2, HALF, TILE), BF),
            pltpu.VMEM((rows, 3, 2, HALF, TILE), BF),
            pltpu.VMEM((512, TILE), F32),
            pltpu.SemaphoreType.DMA((3, 5)),
        ],
        out_shape=[
            jax.ShapeDtypeStruct((1, 2, 128, rows * TILE), BF),
            jax.ShapeDtypeStruct((1, 2, 128, rows * TILE), BF),
            jax.ShapeDtypeStruct((16, 2, 2, 8, 128), F32),
        ],
        compiler_params=params(),
        cost_estimate=pl.CostEstimate(
            flops=2 * 144 * HALF * 512 * 512, bytes_accessed=11 * 2**20, transcendentals=0
        ),
    )(place, coeffs, u_factors, band, up, down)


def on_device(plus_time, minus_time, gate_starts, tile_ranks, u_factors, v_factors):
    u_factors, v_factors, ranks = u_factors[0], v_factors[0], tile_ranks[0].T
    place = lax.axis_index(TILES).astype(jnp.int32).reshape(1)
    rows = make_table(8, 128).astype(F32).transpose(1, 0, 2)
    rows = jnp.broadcast_to(rows[:, :, None], (8, 2, 16, 128)).reshape(256, 128)
    table = jnp.concatenate([rows, rows], axis=1)
    local_spec = dft(plus_time, minus_time, gate_starts.T, table)
    spectra = lax.all_to_all(local_spec, FREQ, 0, 0, tiled=True)
    band, up, down = band_coefficients(spectra, v_factors, ranks, place)
    size = lax.axis_size(TILES)
    from_below = lax.ppermute(down, TILES, [(i, i + 1) for i in range(size - 1)])
    from_above = lax.ppermute(up, TILES, [(i + 1, i) for i in range(size - 1)])
    spectra, band = lax.optimization_barrier((spectra, band))
    coeffs = coefficients(spectra, v_factors, ranks)
    coeffs, from_below, from_above = lax.optimization_barrier((coeffs, from_below, from_above))
    arrived = lax.all_to_all(coeffs, TILES, 0, 0, tiled=True)
    minus_new, plus_new, gram = respond(arrived, u_factors, band, from_below, from_above, place)
    sums = lax.all_to_all(gram, TILES, 0, 0, tiled=True).sum(axis=0)
    return (minus_new, plus_new, sums[None, 0], sums[None, 1])


def solution(mesh):
    torus = Mesh(mesh.devices.reshape(4, 2, 4, 4), (*FREQ, *TILES))
    in_specs = (
        P(FREQ, None, TILES),
        P(FREQ, None, TILES),
        P(FREQ, TILES),
        P(FREQ, None, TILES),
        P(FREQ, TILES, None, None, None, None),
        P(FREQ, None, TILES, None, None, None),
    )
    out_specs = (
        P(FREQ, None, None, TILES),
        P(FREQ, None, None, TILES),
        P(FREQ, None, TILES, None),
        P(FREQ, None, TILES, None),
    )
    return jax.shard_map(
        on_device, mesh=torus, in_specs=in_specs, out_specs=out_specs, check_vma=False
    )
```

```python
import functools
import math

import jax
import jax.numpy as jnp
from jax import lax
from jax.experimental import pallas as pl
from jax.experimental.pallas import tpu as pltpu
from jax.sharding import Mesh
from jax.sharding import PartitionSpec as P

R = 12288
GATE = 64
TILE = 256
HALF = 32
FREQ = ("fx", "fc")
TILES = ("ty", "tz")
BF = jnp.bfloat16
F32 = jnp.float32


def make_table(freq_count, sample_count):
    freq_ids = lax.broadcasted_iota(jnp.int32, (freq_count, sample_count), 0)
    sample_ids = lax.broadcasted_iota(jnp.int32, (freq_count, sample_count), 1)
    phase_ids = freq_ids * sample_ids % sample_count
    angles = phase_ids.astype(F32) * (2.0 * math.pi / sample_count)
    amplitude = 1.0 / math.sqrt(GATE)
    return jnp.stack([jnp.cos(angles) * amplitude, -jnp.sin(angles) * amplitude]).astype(BF)


def params(mib=56):
    return pltpu.CompilerParams(vmem_limit_bytes=mib * 2**20)


def dft_kernel(starts_ref, tab_ref, plus_ref, minus_ref, out_ref, rows_ref, t_ref):
    b = pl.program_id(0)

    @pl.when(b == 0)
    def _():
        rows = jnp.broadcast_to(tab_ref[...][:, None], (16, 16, 128)).reshape(256, 128)
        rows_ref[:, :128] = rows
        rows_ref[:, 128:] = rows

    lane = lax.broadcasted_iota(jnp.int32, (1, 256), 1)
    sample = lane & 127
    upper = lane >= 128
    row_source = lax.broadcasted_iota(jnp.int32, (256, 256), 0) & 15
    for p in range(8):
        start = jnp.where(upper, starts_ref[b, 2 * p + 1], starts_ref[b, 2 * p])
        inside = (sample >= start) & (sample < start + GATE)
        source = jnp.where(inside, jnp.where(upper, 2 * p + 1, 2 * p), -1)
        table = jnp.where(row_source == source, rows_ref[...], 0.0).astype(BF)
        t_ref[:, p * 256 : (p + 1) * 256] = table
    for q, ref in enumerate((plus_ref, minus_ref)):
        prod = jnp.dot(t_ref[...], ref[...].reshape(2048, 256), preferred_element_type=F32)
        prod = prod.reshape(8, 2, 16, 256)
        out_ref[:, 0, q] = prod[:, 0].astype(BF)
        out_ref[:, 1, q] = (prod[:, 1] if q == 0 else -prod[:, 1]).astype(BF)


def dft(plus_time, minus_time, gate_starts, table):
    sources, samples, receivers = plus_time.shape
    blocks = receivers // TILE
    data = pl.BlockSpec((sources, samples, TILE), lambda b: (0, 0, b))
    return pl.pallas_call(
        dft_kernel,
        grid=(blocks,),
        in_specs=[
            pl.BlockSpec(memory_space=pltpu.SMEM),
            pl.BlockSpec((16, 128), lambda b: (0, 0)),
            data,
            data,
        ],
        out_specs=pl.BlockSpec((8, 2, 2, 16, TILE), lambda b: (0, 0, 0, 0, b)),
        out_shape=jax.ShapeDtypeStruct((8, 2, 2, 16, receivers), BF),
        scratch_shapes=[pltpu.VMEM((256, 256), F32), pltpu.VMEM((256, 2048), BF)],
        compiler_params=params(),
        cost_estimate=pl.CostEstimate(
            flops=2 * 2 * 256 * 2048 * receivers, bytes_accessed=7 * 2**20, transcendentals=0
        ),
    )(gate_starts, table, plus_time, minus_time)


def fill_weights(w_ref, x_ref):
    for q in range(2):
        re = x_ref[:, 0, q].reshape(128, TILE).T
        im = x_ref[:, 1, q].reshape(128, TILE).T
        near, far = slice(q * 128, (q + 1) * 128), slice(256 + q * 128, 384 + q * 128)
        w_ref[0:256, near] = re
        w_ref[0:256, far] = im
        w_ref[256:512, near] = -im
        w_ref[256:512, far] = re


def coeff_kernel(
    place_ref, ranks_ref, x_ref, v_hbm, out_hbm, band_ref, v_ref, b_ref, o_ref, e_ref, w_ref, sems
):
    last_row = v_hbm.shape[0] - 1
    owners = out_hbm.shape[0]
    place = place_ref[0]

    def arrivals(j):
        low = v_hbm.at[:, j, :, pl.ds(0, HALF), :]
        copies = [pltpu.make_async_copy(low, v_ref.at[j], sems.at[j, 0])]
        for n in range(3):
            i = jnp.clip(place * 3 + j + n - 1, 0, last_row)
            src = v_hbm.at[i, j, :, pl.ds(HALF, HALF), :]
            copies.append(pltpu.make_async_copy(src, b_ref.at[j, n], sems.at[j, 1 + n]))
        return copies

    def sends(j):
        return [
            pltpu.make_async_copy(o_ref.at[j, i], out_hbm.at[:, 3 * i + j], sems.at[j, 4 + i])
            for i in range(3)
        ]

    def edge(side):
        to = jnp.clip(place + 2 * side - 1, 0, owners - 1)
        return pltpu.make_async_copy(e_ref.at[side], out_hbm.at[to, 9], sems.at[side, 7])

    for copy in arrivals(0):
        copy.start()
    rank_ids = lax.broadcasted_iota(jnp.int32, (HALF, 512), 0)
    band_ref[0, 0] = jnp.zeros((HALF, 512), BF)
    band_ref[2, 2] = jnp.zeros((HALF, 512), BF)
    for j in range(3):
        if j < 2:
            for copy in arrivals(j + 1):
                copy.start()
        fill_weights(w_ref, x_ref.at[:, :, :, :, pl.ds(j * TILE, TILE)])
        for copy in arrivals(j):
            copy.wait()
        v = jnp.concatenate([b_ref[j, :, c].reshape(3 * HALF, TILE) for c in range(2)], axis=1)
        prod = jnp.dot(v, w_ref[...], preferred_element_type=F32)
        for n in range(3):
            i = place * 3 + j + n - 1
            rank = ranks_ref[j, jnp.clip(i, 0, last_row)]
            kept = jnp.where(rank_ids + HALF < rank, prod[n * HALF : (n + 1) * HALF], 0.0).astype(BF)
            il = j + n - 1
            if il < 0:
                e_ref[0] = kept
            elif il > 2:
                e_ref[1] = kept
            else:
                band_ref[il, 2 - n] = kept
        for h in range(4):
            rows = slice(h * 12, (h + 1) * 12)
            v = jnp.concatenate([v_ref[j, rows, c].reshape(12 * HALF, TILE) for c in range(2)], axis=1)
            prod = jnp.dot(v, w_ref[...], preferred_element_type=F32)
            for n in range(12):
                i = h * 12 + n
                kept = jnp.where(rank_ids < ranks_ref[j, i], prod[n * HALF : (n + 1) * HALF], 0.0)
                o_ref[j, i % 3, i // 3] = kept.astype(BF)
        for copy in sends(j):
            copy.start()

    @pl.when(place > 0)
    def _():
        edge(0).start()

    @pl.when(place < owners - 1)
    def _():
        edge(1).start()

    for j in range(3):
        for copy in sends(j):
            copy.wait()

    @pl.when(place > 0)
    def _():
        edge(0).wait()

    @pl.when(place < owners - 1)
    def _():
        edge(1).wait()


def coefficients(spectra, v_factors, ranks, place):
    rows, cols = v_factors.shape[:2]
    whole = pl.BlockSpec(memory_space=pltpu.VMEM)
    scalars = pl.BlockSpec(memory_space=pltpu.SMEM)
    return pl.pallas_call(
        coeff_kernel,
        in_specs=[scalars, scalars, whole, pl.BlockSpec(memory_space=pl.ANY)],
        out_specs=[pl.BlockSpec(memory_space=pl.ANY), whole],
        out_shape=[
            jax.ShapeDtypeStruct((rows // 3, 10, HALF, 512), BF),
            jax.ShapeDtypeStruct((3, 3, HALF, 512), BF),
        ],
        scratch_shapes=[
            pltpu.VMEM((cols, rows, 2, HALF, TILE), BF),
            pltpu.VMEM((cols, 3, 2, HALF, TILE), BF),
            pltpu.VMEM((cols, 3, rows // 3, HALF, 512), BF),
            pltpu.VMEM((2, HALF, 512), BF),
            pltpu.VMEM((512, 512), BF),
            pltpu.SemaphoreType.DMA((3, 8)),
        ],
        compiler_params=params(52),
        cost_estimate=pl.CostEstimate(
            flops=2 * rows * cols * HALF * 512 * 512, bytes_accessed=10 * 2**20, transcendentals=0
        ),
    )(place, ranks, spectra, v_factors)


def response_kernel(
    place_ref, c_hbm, u_hbm, band_ref, minus_hbm, plus_hbm, gram_ref,
    c_ref, u_ref, cb_ref, ub_ref, z_ref, acc, sems,
):
    all_cols = u_hbm.shape[1]
    owners = c_hbm.shape[0]
    place = place_ref[0]
    parts = ((0, owners // 2), (owners // 2, owners - owners // 2))

    def arrivals(i, g):
        first, count = parts[g]
        cols = pl.ds(3 * first, 3 * count)
        pairs = [
            (c_hbm.at[pl.ds(first, count), pl.ds(3 * i, 3)], c_ref.at[i, pl.ds(first, count)]),
            (u_hbm.at[i, cols, :, pl.ds(0, HALF), :], u_ref.at[i, cols]),
        ]
        if g == 1:
            for n in range(3):
                col = jnp.clip(place * 3 + i + n - 1, 0, all_cols - 1)
                pairs.append((u_hbm.at[i, col, :, pl.ds(HALF, HALF), :], ub_ref.at[i, n]))
            if i == 0:
                below = jnp.maximum(place - 1, 0)
                pairs.append((c_hbm.at[below, 9], cb_ref.at[i, 0]))
            if i == 2:
                above = jnp.minimum(place + 1, owners - 1)
                pairs.append((c_hbm.at[above, 9], cb_ref.at[i, 2]))
        at = [2 * g + k for k in range(len(pairs))]
        return [pltpu.make_async_copy(s, d, sems.at[i, k]) for k, (s, d) in zip(at, pairs)]

    def sends(i):
        lanes = pl.ds(i * TILE, TILE)
        return [
            pltpu.make_async_copy(z_ref.at[i, n], ref.at[0, :, :, lanes], sems.at[i, 8 + n])
            for n, ref in enumerate((minus_hbm, plus_hbm))
        ]

    def product(left, right):
        depth = left.shape[0] * HALF
        right = jnp.concatenate([right[:, c].reshape(depth, TILE) for c in range(2)], axis=1)
        left = left.reshape(depth, 512)
        return lax.dot_general(left, right, (((0,), (0,)), ((), ())), preferred_element_type=F32)

    for g in range(2):
        for copy in arrivals(0, g):
            copy.start()
    for i in range(3):
        for n in range(3):
            if (i, n) not in ((0, 0), (2, 2)):
                cb_ref[i, n] = band_ref[i, n]
        cb_ref[i, 3] = jnp.zeros((HALF, 512), BF)
        ub_ref[i, 3] = jnp.zeros((2, HALF, TILE), BF)
    for i in range(3):
        if i < 2:
            for g in range(2):
                for copy in arrivals(i + 1, g):
                    copy.start()
        for copy in arrivals(i, 0):
            copy.wait()
        if i == 0:
            mid = owners // 2
            acc[...] = product(c_ref[0, :mid].reshape(3 * mid, HALF, 512), u_ref[0, : 3 * mid])
        for copy in arrivals(i, 1):
            copy.wait()
        if i == 0:
            cb_ref[0, 0] = jnp.where(place > 0, cb_ref[0, 0], jnp.zeros((), BF))
        if i == 2:
            cb_ref[2, 2] = jnp.where(place < owners - 1, cb_ref[2, 2], jnp.zeros((), BF))
        first = owners // 2 if i == 0 else 0
        prod = product(
            c_ref[i, first:].reshape(3 * (owners - first), HALF, 512), u_ref[i, 3 * first :]
        )
        if i == 0:
            prod += acc[...]
        prod += product(cb_ref[i], ub_ref[i])
        re = (prod[:256, :256] - prod[256:, 256:]).astype(BF)
        im = prod[256:, :256] + prod[:256, 256:]
        im = jnp.concatenate([im[:128], -im[128:]], axis=0).astype(BF)
        z_ref[i, 0, 0] = re[:128]
        z_ref[i, 0, 1] = im[:128]
        z_ref[i, 1, 0] = re[128:]
        z_ref[i, 1, 1] = im[128:]
        for copy in sends(i):
            copy.start()
    rows = [jnp.concatenate([z_ref[i, m, c] for i in range(3)], axis=1) for c in range(2) for m in range(2)]
    gram = lax.dot_general(
        jnp.concatenate(rows, axis=0),
        jnp.concatenate([rows[1], rows[3]], axis=0),
        (((1,), (1,)), ((), ())),
        preferred_element_type=F32,
    )
    parts = (gram[:256, :128] + gram[256:, 128:], gram[256:, :128] - gram[:256, 128:])
    for m, scale in enumerate((1.0 / math.sqrt(R), 1.0 / R)):
        for c, part in enumerate(parts):
            gram_ref[:, m, c] = (part[m * 128 : (m + 1) * 128] * scale).reshape(16, 8, 128)
    for i in range(3):
        for copy in sends(i):
            copy.wait()


def respond(coeffs, u_factors, band, place):
    rows, all_cols = u_factors.shape[:2]
    whole = pl.BlockSpec(memory_space=pltpu.VMEM)
    anywhere = pl.BlockSpec(memory_space=pl.ANY)
    return pl.pallas_call(
        response_kernel,
        in_specs=[pl.BlockSpec(memory_space=pltpu.SMEM), anywhere, anywhere, whole],
        out_specs=[anywhere, anywhere, whole],
        scratch_shapes=[
            pltpu.VMEM((rows, all_cols // 3, 3, HALF, 512), BF),
            pltpu.VMEM((rows, all_cols, 2, HALF, TILE), BF),
            pltpu.VMEM((rows, 4, HALF, 512), BF),
            pltpu.VMEM((rows, 4, 2, HALF, TILE), BF),
            pltpu.VMEM((rows, 2, 2, 128, TILE), BF),
            pltpu.VMEM((512, 512), F32),
            pltpu.SemaphoreType.DMA((3, 10)),
        ],
        out_shape=[
            jax.ShapeDtypeStruct((1, 2, 128, rows * TILE), BF),
            jax.ShapeDtypeStruct((1, 2, 128, rows * TILE), BF),
            jax.ShapeDtypeStruct((16, 2, 2, 8, 128), F32),
        ],
        compiler_params=params(),
        cost_estimate=pl.CostEstimate(
            flops=2 * 144 * HALF * 512 * 512, bytes_accessed=11 * 2**20, transcendentals=0
        ),
    )(place, coeffs, u_factors, band)


def on_device(plus_time, minus_time, gate_starts, tile_ranks, u_factors, v_factors):
    u_factors, v_factors, ranks = u_factors[0], v_factors[0], tile_ranks[0].T
    place = lax.axis_index(TILES).astype(jnp.int32).reshape(1)
    rows = make_table(8, 128).astype(F32).transpose(1, 0, 2)
    local_spec = dft(plus_time, minus_time, gate_starts.T, rows.reshape(16, 128))
    spectra = lax.all_to_all(local_spec, FREQ, 0, 0, tiled=True)
    coeffs, band = coefficients(spectra, v_factors, ranks, place)
    arrived = lax.all_to_all(coeffs, TILES, 0, 0, tiled=True)
    minus_new, plus_new, gram = respond(arrived, u_factors, band, place)
    sums = lax.all_to_all(gram, TILES, 0, 0, tiled=True).sum(axis=0)
    return (minus_new, plus_new, sums[None, 0], sums[None, 1])


def solution(mesh):
    torus = Mesh(mesh.devices.reshape(4, 2, 4, 4), (*FREQ, *TILES))
    in_specs = (
        P(FREQ, None, TILES),
        P(FREQ, None, TILES),
        P(FREQ, TILES),
        P(FREQ, None, TILES),
        P(FREQ, TILES, None, None, None, None),
        P(FREQ, None, TILES, None, None, None),
    )
    out_specs = (
        P(FREQ, None, None, TILES),
        P(FREQ, None, None, TILES),
        P(FREQ, None, TILES, None),
        P(FREQ, None, TILES, None),
    )
    return jax.shard_map(
        on_device, mesh=torus, in_specs=in_specs, out_specs=out_specs, check_vma=False
    )
```

```python
import functools
import math

import jax
import jax.numpy as jnp
from jax import lax
from jax.experimental import pallas as pl
from jax.experimental.pallas import tpu as pltpu
from jax.sharding import Mesh
from jax.sharding import PartitionSpec as P

R = 12288
GATE = 64
TILE = 256
HALF = 32
FREQ = ("fx", "fc")
TILES = ("ty", "tz")
BF = jnp.bfloat16
F32 = jnp.float32


def make_table(freq_count, sample_count):
    freq_ids = lax.broadcasted_iota(jnp.int32, (freq_count, sample_count), 0)
    sample_ids = lax.broadcasted_iota(jnp.int32, (freq_count, sample_count), 1)
    phase_ids = freq_ids * sample_ids % sample_count
    angles = phase_ids.astype(F32) * (2.0 * math.pi / sample_count)
    amplitude = 1.0 / math.sqrt(GATE)
    return jnp.stack([jnp.cos(angles) * amplitude, -jnp.sin(angles) * amplitude]).astype(BF)


def params(mib=56):
    return pltpu.CompilerParams(vmem_limit_bytes=mib * 2**20)


def dft_kernel(starts_ref, tab_ref, plus_ref, minus_ref, out_ref, rows_ref, t_ref):
    b = pl.program_id(0)

    @pl.when(b == 0)
    def _():
        rows = jnp.broadcast_to(tab_ref[...][:, None], (16, 16, 128)).reshape(256, 128)
        rows_ref[:, :128] = rows
        rows_ref[:, 128:] = rows

    lane = lax.broadcasted_iota(jnp.int32, (1, 256), 1)
    sample = lane & 127
    upper = lane >= 128
    row_source = lax.broadcasted_iota(jnp.int32, (256, 256), 0) & 15
    for p in range(8):
        start = jnp.where(upper, starts_ref[b, 2 * p + 1], starts_ref[b, 2 * p])
        inside = (sample >= start) & (sample < start + GATE)
        source = jnp.where(inside, jnp.where(upper, 2 * p + 1, 2 * p), -1)
        table = jnp.where(row_source == source, rows_ref[...], 0.0).astype(BF)
        t_ref[:, p * 256 : (p + 1) * 256] = table
    for q, ref in enumerate((plus_ref, minus_ref)):
        prod = jnp.dot(t_ref[...], ref[...].reshape(2048, 256), preferred_element_type=F32)
        prod = prod.reshape(8, 2, 16, 256)
        out_ref[:, 0, q] = prod[:, 0].astype(BF)
        out_ref[:, 1, q] = (prod[:, 1] if q == 0 else -prod[:, 1]).astype(BF)


def dft(plus_time, minus_time, gate_starts, table):
    sources, samples, receivers = plus_time.shape
    blocks = receivers // TILE
    data = pl.BlockSpec((sources, samples, TILE), lambda b: (0, 0, b))
    return pl.pallas_call(
        dft_kernel,
        grid=(blocks,),
        in_specs=[
            pl.BlockSpec(memory_space=pltpu.SMEM),
            pl.BlockSpec((16, 128), lambda b: (0, 0)),
            data,
            data,
        ],
        out_specs=pl.BlockSpec((8, 2, 2, 16, TILE), lambda b: (0, 0, 0, 0, b)),
        out_shape=jax.ShapeDtypeStruct((8, 2, 2, 16, receivers), BF),
        scratch_shapes=[pltpu.VMEM((256, 256), F32), pltpu.VMEM((256, 2048), BF)],
        compiler_params=params(),
        cost_estimate=pl.CostEstimate(
            flops=2 * 2 * 256 * 2048 * receivers, bytes_accessed=7 * 2**20, transcendentals=0
        ),
    )(gate_starts, table, plus_time, minus_time)


def hold_kernel(u_hbm, u_ref, sem):
    copy = pltpu.make_async_copy(u_hbm.at[:, :, :, pl.ds(0, HALF), :], u_ref, sem)
    copy.start()
    copy.wait()


def held(u_factors):
    return pl.pallas_call(
        hold_kernel,
        in_specs=[pl.BlockSpec(memory_space=pl.ANY)],
        out_specs=pl.BlockSpec(memory_space=pltpu.VMEM),
        out_shape=pltpu.VMEM((*u_factors.shape[:3], HALF, TILE), BF),
        scratch_shapes=[pltpu.SemaphoreType.DMA],
        compiler_params=params(52),
        cost_estimate=pl.CostEstimate(flops=0, bytes_accessed=5 * 2**20, transcendentals=0),
    )(u_factors)


def fill_weights(w_ref, x_ref):
    for q in range(2):
        re = x_ref[:, 0, q].reshape(128, TILE).T
        im = x_ref[:, 1, q].reshape(128, TILE).T
        near, far = slice(q * 128, (q + 1) * 128), slice(256 + q * 128, 384 + q * 128)
        w_ref[0:256, near] = re
        w_ref[0:256, far] = im
        w_ref[256:512, near] = -im
        w_ref[256:512, far] = re


def coeff_kernel(
    place_ref, ranks_ref, x_ref, v_hbm, out_hbm, band_ref, v_ref, b_ref, o_ref, e_ref, w_ref, sems
):
    last_row = v_hbm.shape[0] - 1
    owners = out_hbm.shape[0]
    place = place_ref[0]

    def arrivals(j):
        low = v_hbm.at[:, j, :, pl.ds(0, HALF), :]
        copies = [pltpu.make_async_copy(low, v_ref.at[j], sems.at[j, 0])]
        for n in range(3):
            i = jnp.clip(place * 3 + j + n - 1, 0, last_row)
            src = v_hbm.at[i, j, :, pl.ds(HALF, HALF), :]
            copies.append(pltpu.make_async_copy(src, b_ref.at[j, n], sems.at[j, 1 + n]))
        return copies

    def sends(j):
        return [
            pltpu.make_async_copy(o_ref.at[j, i], out_hbm.at[:, 3 * i + j], sems.at[j, 4 + i])
            for i in range(3)
        ]

    def edge(side):
        to = jnp.clip(place + 2 * side - 1, 0, owners - 1)
        return pltpu.make_async_copy(e_ref.at[side], out_hbm.at[to, 9], sems.at[side, 7])

    for copy in arrivals(0):
        copy.start()
    rank_ids = lax.broadcasted_iota(jnp.int32, (HALF, 512), 0)
    band_ref[0, 0] = jnp.zeros((HALF, 512), BF)
    band_ref[2, 2] = jnp.zeros((HALF, 512), BF)
    for j in range(3):
        if j < 2:
            for copy in arrivals(j + 1):
                copy.start()
        fill_weights(w_ref, x_ref.at[:, :, :, :, pl.ds(j * TILE, TILE)])
        for copy in arrivals(j):
            copy.wait()
        v = jnp.concatenate([b_ref[j, :, c].reshape(3 * HALF, TILE) for c in range(2)], axis=1)
        prod = jnp.dot(v, w_ref[...], preferred_element_type=F32)
        for n in range(3):
            i = place * 3 + j + n - 1
            rank = ranks_ref[j, jnp.clip(i, 0, last_row)]
            kept = jnp.where(rank_ids + HALF < rank, prod[n * HALF : (n + 1) * HALF], 0.0).astype(BF)
            il = j + n - 1
            if il < 0:
                e_ref[0] = kept
            elif il > 2:
                e_ref[1] = kept
            else:
                band_ref[il, 2 - n] = kept
        for h in range(4):
            rows = slice(h * 12, (h + 1) * 12)
            v = jnp.concatenate([v_ref[j, rows, c].reshape(12 * HALF, TILE) for c in range(2)], axis=1)
            prod = jnp.dot(v, w_ref[...], preferred_element_type=F32)
            for n in range(12):
                i = h * 12 + n
                kept = jnp.where(rank_ids < ranks_ref[j, i], prod[n * HALF : (n + 1) * HALF], 0.0)
                o_ref[j, i % 3, i // 3] = kept.astype(BF)
        for copy in sends(j):
            copy.start()

    @pl.when(place > 0)
    def _():
        edge(0).start()

    @pl.when(place < owners - 1)
    def _():
        edge(1).start()

    for j in range(3):
        for copy in sends(j):
            copy.wait()

    @pl.when(place > 0)
    def _():
        edge(0).wait()

    @pl.when(place < owners - 1)
    def _():
        edge(1).wait()


def coefficients(spectra, v_factors, ranks, place):
    rows, cols = v_factors.shape[:2]
    whole = pl.BlockSpec(memory_space=pltpu.VMEM)
    scalars = pl.BlockSpec(memory_space=pltpu.SMEM)
    return pl.pallas_call(
        coeff_kernel,
        in_specs=[scalars, scalars, whole, pl.BlockSpec(memory_space=pl.ANY)],
        out_specs=[pl.BlockSpec(memory_space=pl.ANY), whole],
        out_shape=[
            jax.ShapeDtypeStruct((rows // 3, 10, HALF, 512), BF),
            jax.ShapeDtypeStruct((3, 3, HALF, 512), BF),
        ],
        scratch_shapes=[
            pltpu.VMEM((cols, rows, 2, HALF, TILE), BF),
            pltpu.VMEM((cols, 3, 2, HALF, TILE), BF),
            pltpu.VMEM((cols, 3, rows // 3, HALF, 512), BF),
            pltpu.VMEM((2, HALF, 512), BF),
            pltpu.VMEM((512, 512), BF),
            pltpu.SemaphoreType.DMA((3, 8)),
        ],
        compiler_params=params(52),
        cost_estimate=pl.CostEstimate(
            flops=2 * rows * cols * HALF * 512 * 512, bytes_accessed=10 * 2**20, transcendentals=0
        ),
    )(place, ranks, spectra, v_factors)


def response_kernel(
    place_ref, c_hbm, u_ref, u_hbm, band_ref, minus_hbm, plus_hbm, gram_ref,
    c_ref, cb_ref, ub_ref, z_ref, acc, sems,
):
    all_cols = u_hbm.shape[1]
    owners = c_hbm.shape[0]
    place = place_ref[0]
    parts = ((0, owners // 2), (owners // 2, owners - owners // 2))

    def arrivals(i, g):
        first, count = parts[g]
        pairs = [
            (c_hbm.at[pl.ds(first, count), pl.ds(3 * i, 3)], c_ref.at[i, pl.ds(first, count)]),
        ]
        if g == 1:
            for n in range(3):
                col = jnp.clip(place * 3 + i + n - 1, 0, all_cols - 1)
                pairs.append((u_hbm.at[i, col, :, pl.ds(HALF, HALF), :], ub_ref.at[i, n]))
            if i == 0:
                below = jnp.maximum(place - 1, 0)
                pairs.append((c_hbm.at[below, 9], cb_ref.at[i, 0]))
            if i == 2:
                above = jnp.minimum(place + 1, owners - 1)
                pairs.append((c_hbm.at[above, 9], cb_ref.at[i, 2]))
        at = [2 * g + k for k in range(len(pairs))]
        return [pltpu.make_async_copy(s, d, sems.at[i, k]) for k, (s, d) in zip(at, pairs)]

    def sends(i):
        lanes = pl.ds(i * TILE, TILE)
        return [
            pltpu.make_async_copy(z_ref.at[i, n], ref.at[0, :, :, lanes], sems.at[i, 8 + n])
            for n, ref in enumerate((minus_hbm, plus_hbm))
        ]

    def product(left, right):
        depth = left.shape[0] * HALF
        right = jnp.concatenate([right[:, c].reshape(depth, TILE) for c in range(2)], axis=1)
        left = left.reshape(depth, 512)
        return lax.dot_general(left, right, (((0,), (0,)), ((), ())), preferred_element_type=F32)

    for g in range(2):
        for copy in arrivals(0, g):
            copy.start()
    for i in range(3):
        for n in range(3):
            if (i, n) not in ((0, 0), (2, 2)):
                cb_ref[i, n] = band_ref[i, n]
        cb_ref[i, 3] = jnp.zeros((HALF, 512), BF)
        ub_ref[i, 3] = jnp.zeros((2, HALF, TILE), BF)
    for i in range(3):
        if i < 2:
            for g in range(2):
                for copy in arrivals(i + 1, g):
                    copy.start()
        for copy in arrivals(i, 0):
            copy.wait()
        if i == 0:
            mid = owners // 2
            acc[...] = product(c_ref[0, :mid].reshape(3 * mid, HALF, 512), u_ref[0, : 3 * mid])
        for copy in arrivals(i, 1):
            copy.wait()
        if i == 0:
            cb_ref[0, 0] = jnp.where(place > 0, cb_ref[0, 0], jnp.zeros((), BF))
        if i == 2:
            cb_ref[2, 2] = jnp.where(place < owners - 1, cb_ref[2, 2], jnp.zeros((), BF))
        first = owners // 2 if i == 0 else 0
        prod = product(
            c_ref[i, first:].reshape(3 * (owners - first), HALF, 512), u_ref[i, 3 * first :]
        )
        if i == 0:
            prod += acc[...]
        prod += product(cb_ref[i], ub_ref[i])
        re = (prod[:256, :256] - prod[256:, 256:]).astype(BF)
        im = prod[256:, :256] + prod[:256, 256:]
        im = jnp.concatenate([im[:128], -im[128:]], axis=0).astype(BF)
        z_ref[i, 0, 0] = re[:128]
        z_ref[i, 0, 1] = im[:128]
        z_ref[i, 1, 0] = re[128:]
        z_ref[i, 1, 1] = im[128:]
        for copy in sends(i):
            copy.start()
    rows = [jnp.concatenate([z_ref[i, m, c] for i in range(3)], axis=1) for c in range(2) for m in range(2)]
    gram = lax.dot_general(
        jnp.concatenate(rows, axis=0),
        jnp.concatenate([rows[1], rows[3]], axis=0),
        (((1,), (1,)), ((), ())),
        preferred_element_type=F32,
    )
    parts = (gram[:256, :128] + gram[256:, 128:], gram[256:, :128] - gram[:256, 128:])
    for m, scale in enumerate((1.0 / math.sqrt(R), 1.0 / R)):
        for c, part in enumerate(parts):
            gram_ref[:, m, c] = (part[m * 128 : (m + 1) * 128] * scale).reshape(16, 8, 128)
    for i in range(3):
        for copy in sends(i):
            copy.wait()


def respond(coeffs, u_held, u_factors, band, place):
    rows, all_cols = u_factors.shape[:2]
    whole = pl.BlockSpec(memory_space=pltpu.VMEM)
    anywhere = pl.BlockSpec(memory_space=pl.ANY)
    return pl.pallas_call(
        response_kernel,
        in_specs=[pl.BlockSpec(memory_space=pltpu.SMEM), anywhere, whole, anywhere, whole],
        out_specs=[anywhere, anywhere, whole],
        scratch_shapes=[
            pltpu.VMEM((rows, all_cols // 3, 3, HALF, 512), BF),
            pltpu.VMEM((rows, 4, HALF, 512), BF),
            pltpu.VMEM((rows, 4, 2, HALF, TILE), BF),
            pltpu.VMEM((rows, 2, 2, 128, TILE), BF),
            pltpu.VMEM((512, 512), F32),
            pltpu.SemaphoreType.DMA((3, 10)),
        ],
        out_shape=[
            jax.ShapeDtypeStruct((1, 2, 128, rows * TILE), BF),
            jax.ShapeDtypeStruct((1, 2, 128, rows * TILE), BF),
            jax.ShapeDtypeStruct((16, 2, 2, 8, 128), F32),
        ],
        compiler_params=params(40),
        cost_estimate=pl.CostEstimate(
            flops=2 * 144 * HALF * 512 * 512, bytes_accessed=11 * 2**20, transcendentals=0
        ),
    )(place, coeffs, u_held, u_factors, band)


def on_device(plus_time, minus_time, gate_starts, tile_ranks, u_factors, v_factors):
    u_factors, v_factors, ranks = u_factors[0], v_factors[0], tile_ranks[0].T
    place = lax.axis_index(TILES).astype(jnp.int32).reshape(1)
    rows = make_table(8, 128).astype(F32).transpose(1, 0, 2)
    local_spec = dft(plus_time, minus_time, gate_starts.T, rows.reshape(16, 128))
    spectra = lax.all_to_all(local_spec, FREQ, 0, 0, tiled=True)
    spectra, u_held = lax.optimization_barrier((spectra, held(u_factors)))
    coeffs, band = coefficients(spectra, v_factors, ranks, place)
    arrived = lax.all_to_all(coeffs, TILES, 0, 0, tiled=True)
    minus_new, plus_new, gram = respond(arrived, u_held, u_factors, band, place)
    sums = lax.all_to_all(gram, TILES, 0, 0, tiled=True).sum(axis=0)
    return (minus_new, plus_new, sums[None, 0], sums[None, 1])


def solution(mesh):
    torus = Mesh(mesh.devices.reshape(4, 2, 4, 4), (*FREQ, *TILES))
    in_specs = (
        P(FREQ, None, TILES),
        P(FREQ, None, TILES),
        P(FREQ, TILES),
        P(FREQ, None, TILES),
        P(FREQ, TILES, None, None, None, None),
        P(FREQ, None, TILES, None, None, None),
    )
    out_specs = (
        P(FREQ, None, None, TILES),
        P(FREQ, None, None, TILES),
        P(FREQ, None, TILES, None),
        P(FREQ, None, TILES, None),
    )
    return jax.shard_map(
        on_device, mesh=torus, in_specs=in_specs, out_specs=out_specs, check_vma=False
    )
```

```python
import functools
import math

import jax
import jax.numpy as jnp
from jax import lax
from jax.experimental import pallas as pl
from jax.experimental.pallas import tpu as pltpu
from jax.sharding import Mesh
from jax.sharding import PartitionSpec as P

R = 12288
GATE = 64
TILE = 256
HALF = 32
FREQ = ("fx", "fc")
TILES = ("ty", "tz")
BF = jnp.bfloat16
F32 = jnp.float32


def make_table(freq_count, sample_count):
    row_ids = lax.broadcasted_iota(jnp.int32, (2 * freq_count, sample_count), 0)
    sample_ids = lax.broadcasted_iota(jnp.int32, (2 * freq_count, sample_count), 1)
    phase_ids = row_ids // 2 * sample_ids % sample_count
    angles = phase_ids.astype(F32) * (2.0 * math.pi / sample_count)
    amplitude = 1.0 / math.sqrt(GATE)
    return jnp.where(
        row_ids % 2 == 0, jnp.cos(angles) * amplitude, -jnp.sin(angles) * amplitude
    ).astype(BF)


def params(mib=56):
    return pltpu.CompilerParams(vmem_limit_bytes=mib * 2**20)


def dft_kernel(starts_ref, tab_ref, plus_ref, minus_ref, out_ref, rows_ref, t_ref):
    b = pl.program_id(0)

    @pl.when(b == 0)
    def _():
        rows = jnp.broadcast_to(tab_ref[...][:, None], (16, 16, 128)).reshape(256, 128)
        rows_ref[:, :128] = rows
        rows_ref[:, 128:] = rows

    lane = lax.broadcasted_iota(jnp.int32, (1, 256), 1)
    sample = lane & 127
    upper = lane >= 128
    row_source = lax.broadcasted_iota(jnp.int32, (256, 256), 0) & 15
    for p in range(8):
        start = jnp.where(upper, starts_ref[b, 2 * p + 1], starts_ref[b, 2 * p])
        inside = (sample >= start) & (sample < start + GATE)
        source = jnp.where(inside, jnp.where(upper, 2 * p + 1, 2 * p), -1)
        table = jnp.where(row_source == source, rows_ref[...], 0.0).astype(BF)
        t_ref[:, p * 256 : (p + 1) * 256] = table
    for q, ref in enumerate((plus_ref, minus_ref)):
        prod = jnp.dot(t_ref[...], ref[...].reshape(2048, 256), preferred_element_type=F32)
        prod = prod.reshape(8, 2, 16, 256)
        out_ref[:, 0, q] = prod[:, 0].astype(BF)
        out_ref[:, 1, q] = (prod[:, 1] if q == 0 else -prod[:, 1]).astype(BF)


def dft(plus_time, minus_time, gate_starts, table):
    sources, samples, receivers = plus_time.shape
    blocks = receivers // TILE
    data = pl.BlockSpec((sources, samples, TILE), lambda b: (0, 0, b))
    return pl.pallas_call(
        dft_kernel,
        grid=(blocks,),
        in_specs=[
            pl.BlockSpec(memory_space=pltpu.SMEM),
            pl.BlockSpec((16, 128), lambda b: (0, 0)),
            data,
            data,
        ],
        out_specs=pl.BlockSpec((8, 2, 2, 16, TILE), lambda b: (0, 0, 0, 0, b)),
        out_shape=jax.ShapeDtypeStruct((8, 2, 2, 16, receivers), BF),
        scratch_shapes=[pltpu.VMEM((256, 256), F32), pltpu.VMEM((256, 2048), BF)],
        compiler_params=params(),
        cost_estimate=pl.CostEstimate(
            flops=2 * 2 * 256 * 2048 * receivers, bytes_accessed=7 * 2**20, transcendentals=0
        ),
    )(gate_starts, table, plus_time, minus_time)


def hold_kernel(u_hbm, u_ref, sem):
    copy = pltpu.make_async_copy(u_hbm.at[:, :, :, pl.ds(0, HALF), :], u_ref, sem)
    copy.start()
    copy.wait()


def held(u_factors):
    return pl.pallas_call(
        hold_kernel,
        in_specs=[pl.BlockSpec(memory_space=pl.ANY)],
        out_specs=pl.BlockSpec(memory_space=pltpu.VMEM),
        out_shape=pltpu.VMEM((*u_factors.shape[:3], HALF, TILE), BF),
        scratch_shapes=[pltpu.SemaphoreType.DMA],
        compiler_params=params(52),
        cost_estimate=pl.CostEstimate(flops=0, bytes_accessed=5 * 2**20, transcendentals=0),
    )(u_factors)


def fill_weights(w_ref, x_ref):
    for q in range(2):
        re = x_ref[:, 0, q].reshape(128, TILE).T
        im = x_ref[:, 1, q].reshape(128, TILE).T
        near, far = slice(q * 128, (q + 1) * 128), slice(256 + q * 128, 384 + q * 128)
        w_ref[0:256, near] = re
        w_ref[0:256, far] = im
        w_ref[256:512, near] = -im
        w_ref[256:512, far] = re


def coeff_kernel(
    place_ref, ranks_ref, x_ref, v_hbm, out_hbm, band_ref, v_ref, b_ref, o_ref, e_ref, w_ref, sems
):
    last_row = v_hbm.shape[0] - 1
    owners = out_hbm.shape[0]
    place = place_ref[0]

    def arrivals(j):
        low = v_hbm.at[:, j, :, pl.ds(0, HALF), :]
        copies = [pltpu.make_async_copy(low, v_ref.at[j], sems.at[j, 0])]
        for n in range(3):
            i = jnp.clip(place * 3 + j + n - 1, 0, last_row)
            src = v_hbm.at[i, j, :, pl.ds(HALF, HALF), :]
            copies.append(pltpu.make_async_copy(src, b_ref.at[j, n], sems.at[j, 1 + n]))
        return copies

    def sends(j):
        return [
            pltpu.make_async_copy(o_ref.at[j, i], out_hbm.at[:, 3 * i + j], sems.at[j, 4 + i])
            for i in range(3)
        ]

    def edge(side):
        to = jnp.clip(place + 2 * side - 1, 0, owners - 1)
        return pltpu.make_async_copy(e_ref.at[side], out_hbm.at[to, 9], sems.at[side, 7])

    for copy in arrivals(0):
        copy.start()
    rank_ids = lax.broadcasted_iota(jnp.int32, (HALF, 512), 0)
    band_ref[0, 0] = jnp.zeros((HALF, 512), BF)
    band_ref[2, 2] = jnp.zeros((HALF, 512), BF)
    for j in range(3):
        if j < 2:
            for copy in arrivals(j + 1):
                copy.start()
        fill_weights(w_ref, x_ref.at[:, :, :, :, pl.ds(j * TILE, TILE)])
        for copy in arrivals(j):
            copy.wait()
        v = jnp.concatenate([b_ref[j, :, c].reshape(3 * HALF, TILE) for c in range(2)], axis=1)
        prod = jnp.dot(v, w_ref[...], preferred_element_type=F32)
        for n in range(3):
            i = place * 3 + j + n - 1
            rank = ranks_ref[j, jnp.clip(i, 0, last_row)]
            kept = jnp.where(rank_ids + HALF < rank, prod[n * HALF : (n + 1) * HALF], 0.0).astype(BF)
            il = j + n - 1
            if il < 0:
                e_ref[0] = kept
            elif il > 2:
                e_ref[1] = kept
            else:
                band_ref[il, 2 - n] = kept
        for h in range(4):
            rows = slice(h * 12, (h + 1) * 12)
            v = jnp.concatenate([v_ref[j, rows, c].reshape(12 * HALF, TILE) for c in range(2)], axis=1)
            prod = jnp.dot(v, w_ref[...], preferred_element_type=F32)
            for n in range(12):
                i = h * 12 + n
                kept = jnp.where(rank_ids < ranks_ref[j, i], prod[n * HALF : (n + 1) * HALF], 0.0)
                o_ref[j, i % 3, i // 3] = kept.astype(BF)
        for copy in sends(j):
            copy.start()

    @pl.when(place > 0)
    def _():
        edge(0).start()

    @pl.when(place < owners - 1)
    def _():
        edge(1).start()

    for j in range(3):
        for copy in sends(j):
            copy.wait()

    @pl.when(place > 0)
    def _():
        edge(0).wait()

    @pl.when(place < owners - 1)
    def _():
        edge(1).wait()


def coefficients(spectra, v_factors, ranks, place):
    rows, cols = v_factors.shape[:2]
    whole = pl.BlockSpec(memory_space=pltpu.VMEM)
    scalars = pl.BlockSpec(memory_space=pltpu.SMEM)
    return pl.pallas_call(
        coeff_kernel,
        in_specs=[scalars, scalars, whole, pl.BlockSpec(memory_space=pl.ANY)],
        out_specs=[pl.BlockSpec(memory_space=pl.ANY), whole],
        out_shape=[
            jax.ShapeDtypeStruct((rows // 3, 10, HALF, 512), BF),
            jax.ShapeDtypeStruct((3, 3, HALF, 512), BF),
        ],
        scratch_shapes=[
            pltpu.VMEM((cols, rows, 2, HALF, TILE), BF),
            pltpu.VMEM((cols, 3, 2, HALF, TILE), BF),
            pltpu.VMEM((cols, 3, rows // 3, HALF, 512), BF),
            pltpu.VMEM((2, HALF, 512), BF),
            pltpu.VMEM((512, 512), BF),
            pltpu.SemaphoreType.DMA((3, 8)),
        ],
        compiler_params=params(52),
        cost_estimate=pl.CostEstimate(
            flops=2 * rows * cols * HALF * 512 * 512, bytes_accessed=10 * 2**20, transcendentals=0
        ),
    )(place, ranks, spectra, v_factors)


def response_kernel(
    place_ref, c_ref, u_ref, u_hbm, band_ref, minus_hbm, plus_hbm, gram_ref, cb_ref, ub_ref, z_ref, sems
):
    all_cols = u_hbm.shape[1]
    owners = c_ref.shape[0]
    place = place_ref[0]

    def arrivals(i):
        cols = [jnp.clip(place * 3 + i + n - 1, 0, all_cols - 1) for n in range(3)]
        return [
            pltpu.make_async_copy(
                u_hbm.at[i, cols[n], :, pl.ds(HALF, HALF), :], ub_ref.at[i, n], sems.at[i, n]
            )
            for n in range(3)
        ]

    def sends(i):
        lanes = pl.ds(i * TILE, TILE)
        return [
            pltpu.make_async_copy(z_ref.at[i, n], ref.at[0, :, :, lanes], sems.at[i, 3 + n])
            for n, ref in enumerate((minus_hbm, plus_hbm))
        ]

    def product(left, right):
        depth = left.shape[0] * HALF
        right = jnp.concatenate([right[:, c].reshape(depth, TILE) for c in range(2)], axis=1)
        left = left.reshape(depth, 512)
        return lax.dot_general(left, right, (((0,), (0,)), ((), ())), preferred_element_type=F32)

    for i in range(3):
        for copy in arrivals(i):
            copy.start()
    below = c_ref[jnp.maximum(place - 1, 0), 9]
    above = c_ref[jnp.minimum(place + 1, owners - 1), 9]
    for i in range(3):
        for n in range(3):
            cb_ref[i, n] = band_ref[i, n]
        cb_ref[i, 3] = jnp.zeros((HALF, 512), BF)
        ub_ref[i, 3] = jnp.zeros((2, HALF, TILE), BF)
    cb_ref[0, 0] = jnp.where(place > 0, below, jnp.zeros((), BF))
    cb_ref[2, 2] = jnp.where(place < owners - 1, above, jnp.zeros((), BF))
    for i in range(3):
        prod = product(c_ref[:, 3 * i : 3 * i + 3].reshape(3 * owners, HALF, 512), u_ref[i])
        for copy in arrivals(i):
            copy.wait()
        prod += product(cb_ref[i], ub_ref[i])
        re = (prod[:256, :256] - prod[256:, 256:]).astype(BF)
        im = prod[256:, :256] + prod[:256, 256:]
        im = jnp.concatenate([im[:128], -im[128:]], axis=0).astype(BF)
        z_ref[i, 0, 0] = re[:128]
        z_ref[i, 0, 1] = im[:128]
        z_ref[i, 1, 0] = re[128:]
        z_ref[i, 1, 1] = im[128:]
        for copy in sends(i):
            copy.start()
    rows = [jnp.concatenate([z_ref[i, m, c] for i in range(3)], axis=1) for c in range(2) for m in range(2)]
    gram = lax.dot_general(
        jnp.concatenate(rows, axis=0),
        jnp.concatenate([rows[1], rows[3]], axis=0),
        (((1,), (1,)), ((), ())),
        preferred_element_type=F32,
    )
    parts = (gram[:256, :128] + gram[256:, 128:], gram[256:, :128] - gram[:256, 128:])
    for m, scale in enumerate((1.0 / math.sqrt(R), 1.0 / R)):
        for c, part in enumerate(parts):
            gram_ref[:, m, c] = (part[m * 128 : (m + 1) * 128] * scale).reshape(16, 8, 128)
    for i in range(3):
        for copy in sends(i):
            copy.wait()


def respond(coeffs, u_held, u_factors, band, place):
    rows, all_cols = u_factors.shape[:2]
    whole = pl.BlockSpec(memory_space=pltpu.VMEM)
    anywhere = pl.BlockSpec(memory_space=pl.ANY)
    return pl.pallas_call(
        response_kernel,
        in_specs=[pl.BlockSpec(memory_space=pltpu.SMEM), whole, whole, anywhere, whole],
        out_specs=[anywhere, anywhere, whole],
        scratch_shapes=[
            pltpu.VMEM((rows, 4, HALF, 512), BF),
            pltpu.VMEM((rows, 4, 2, HALF, TILE), BF),
            pltpu.VMEM((rows, 2, 2, 128, TILE), BF),
            pltpu.SemaphoreType.DMA((3, 5)),
        ],
        out_shape=[
            jax.ShapeDtypeStruct((1, 2, 128, rows * TILE), BF),
            jax.ShapeDtypeStruct((1, 2, 128, rows * TILE), BF),
            jax.ShapeDtypeStruct((16, 2, 2, 8, 128), F32),
        ],
        compiler_params=params(40),
        cost_estimate=pl.CostEstimate(
            flops=2 * 144 * HALF * 512 * 512, bytes_accessed=11 * 2**20, transcendentals=0
        ),
    )(place, coeffs, u_held, u_factors, band)


def on_device(plus_time, minus_time, gate_starts, tile_ranks, u_factors, v_factors):
    u_factors, v_factors, ranks = u_factors[0], v_factors[0], tile_ranks[0].T
    place = lax.axis_index(TILES).astype(jnp.int32).reshape(1)
    local_spec = dft(plus_time, minus_time, gate_starts.T, make_table(8, 128).astype(F32))
    spectra = lax.all_to_all(local_spec, FREQ, 0, 0, tiled=True)
    spectra, u_held = lax.optimization_barrier((spectra, held(u_factors)))
    coeffs, band = coefficients(spectra, v_factors, ranks, place)
    arrived = lax.all_to_all(coeffs, TILES, 0, 0, tiled=True)
    minus_new, plus_new, gram = respond(arrived, u_held, u_factors, band, place)
    sums = lax.all_to_all(gram, TILES, 0, 0, tiled=True).sum(axis=0)
    return (minus_new, plus_new, sums[None, 0], sums[None, 1])


def solution(mesh):
    torus = Mesh(mesh.devices.reshape(4, 2, 4, 4), (*FREQ, *TILES))
    in_specs = (
        P(FREQ, None, TILES),
        P(FREQ, None, TILES),
        P(FREQ, TILES),
        P(FREQ, None, TILES),
        P(FREQ, TILES, None, None, None, None),
        P(FREQ, None, TILES, None, None, None),
    )
    out_specs = (
        P(FREQ, None, None, TILES),
        P(FREQ, None, None, TILES),
        P(FREQ, None, TILES, None),
        P(FREQ, None, TILES, None),
    )
    return jax.shard_map(
        on_device, mesh=torus, in_specs=in_specs, out_specs=out_specs, check_vma=False
    )
```

```python
import functools
import math

import jax
import jax.numpy as jnp
from jax import lax
from jax.experimental import pallas as pl
from jax.experimental.pallas import tpu as pltpu
from jax.sharding import Mesh
from jax.sharding import PartitionSpec as P

R = 12288
GATE = 64
TILE = 256
HALF = 32
FREQ = ("fx", "fc")
TILES = ("ty", "tz")
BF = jnp.bfloat16
F32 = jnp.float32


def make_table(freq_count, sample_count):
    row_ids = lax.broadcasted_iota(jnp.int32, (2 * freq_count, sample_count), 0)
    sample_ids = lax.broadcasted_iota(jnp.int32, (2 * freq_count, sample_count), 1)
    phase_ids = row_ids // 2 * sample_ids % sample_count
    angles = phase_ids.astype(F32) * (2.0 * math.pi / sample_count)
    amplitude = 1.0 / math.sqrt(GATE)
    return jnp.where(
        row_ids % 2 == 0, jnp.cos(angles) * amplitude, -jnp.sin(angles) * amplitude
    ).astype(BF)


def params(mib=56):
    return pltpu.CompilerParams(vmem_limit_bytes=mib * 2**20)


def dft_kernel(starts_ref, tab_ref, plus_ref, minus_ref, out_ref, rows_ref, t_ref):
    b = pl.program_id(0)

    @pl.when(b == 0)
    def _():
        rows = jnp.broadcast_to(tab_ref[...][:, None], (16, 16, 128)).reshape(256, 128)
        rows_ref[:, :128] = rows
        rows_ref[:, 128:] = rows

    lane = lax.broadcasted_iota(jnp.int32, (1, 256), 1)
    sample = lane & 127
    upper = lane >= 128
    row_source = lax.broadcasted_iota(jnp.int32, (256, 256), 0) & 15
    for p in range(8):
        start = jnp.where(upper, starts_ref[b, 2 * p + 1], starts_ref[b, 2 * p])
        inside = (sample >= start) & (sample < start + GATE)
        source = jnp.where(inside, jnp.where(upper, 2 * p + 1, 2 * p), -1)
        table = jnp.where(row_source == source, rows_ref[...], 0.0).astype(BF)
        t_ref[:, p * 256 : (p + 1) * 256] = table
    for q, ref in enumerate((plus_ref, minus_ref)):
        prod = jnp.dot(t_ref[...], ref[...].reshape(2048, 256), preferred_element_type=F32)
        prod = prod.reshape(8, 2, 16, 256)
        out_ref[:, 0, q] = prod[:, 0].astype(BF)
        out_ref[:, 1, q] = (prod[:, 1] if q == 0 else -prod[:, 1]).astype(BF)


def dft(plus_time, minus_time, gate_starts, table):
    sources, samples, receivers = plus_time.shape
    blocks = receivers // TILE
    data = pl.BlockSpec((sources, samples, TILE), lambda b: (0, 0, b))
    return pl.pallas_call(
        dft_kernel,
        grid=(blocks,),
        in_specs=[
            pl.BlockSpec(memory_space=pltpu.SMEM),
            pl.BlockSpec((16, 128), lambda b: (0, 0)),
            data,
            data,
        ],
        out_specs=pl.BlockSpec((8, 2, 2, 16, TILE), lambda b: (0, 0, 0, 0, b)),
        out_shape=jax.ShapeDtypeStruct((8, 2, 2, 16, receivers), BF),
        scratch_shapes=[pltpu.VMEM((256, 256), F32), pltpu.VMEM((256, 2048), BF)],
        compiler_params=params(),
        cost_estimate=pl.CostEstimate(
            flops=2 * 2 * 256 * 2048 * receivers, bytes_accessed=7 * 2**20, transcendentals=0
        ),
    )(gate_starts, table, plus_time, minus_time)


def hold_kernel(u_hbm, u_ref, sem):
    copy = pltpu.make_async_copy(u_hbm.at[:, :, :, pl.ds(0, HALF), :], u_ref, sem)
    copy.start()
    copy.wait()


def held(u_factors):
    return pl.pallas_call(
        hold_kernel,
        in_specs=[pl.BlockSpec(memory_space=pl.ANY)],
        out_specs=pl.BlockSpec(memory_space=pltpu.VMEM),
        out_shape=pltpu.VMEM((*u_factors.shape[:3], HALF, TILE), BF),
        scratch_shapes=[pltpu.SemaphoreType.DMA],
        compiler_params=params(52),
        cost_estimate=pl.CostEstimate(flops=0, bytes_accessed=5 * 2**20, transcendentals=0),
    )(u_factors)


def fill_weights(w_ref, x_ref):
    for q in range(2):
        re = x_ref[:, 0, q].reshape(128, TILE).T
        im = x_ref[:, 1, q].reshape(128, TILE).T
        near, far = slice(q * 128, (q + 1) * 128), slice(256 + q * 128, 384 + q * 128)
        w_ref[0:256, near] = re
        w_ref[0:256, far] = im
        w_ref[256:512, near] = -im
        w_ref[256:512, far] = re


def coeff_kernel(
    place_ref, ranks_ref, x_ref, v_hbm, out_hbm, band_ref, v_ref, b_ref, o_ref, e_ref, w_ref, sems
):
    last_row = v_hbm.shape[0] - 1
    owners = out_hbm.shape[0]
    place = place_ref[0]

    def arrivals(j):
        low = v_hbm.at[:, j, :, pl.ds(0, HALF), :]
        copies = [pltpu.make_async_copy(low, v_ref.at[j], sems.at[j, 0])]
        for n in range(3):
            i = jnp.clip(place * 3 + j + n - 1, 0, last_row)
            src = v_hbm.at[i, j, :, pl.ds(HALF, HALF), :]
            copies.append(pltpu.make_async_copy(src, b_ref.at[j, n], sems.at[j, 1 + n]))
        return copies

    def sends(j):
        return [
            pltpu.make_async_copy(o_ref.at[j, i], out_hbm.at[:, 3 * i + j], sems.at[j, 4 + i])
            for i in range(3)
        ]

    def edge(side):
        to = jnp.clip(place + 2 * side - 1, 0, owners - 1)
        return pltpu.make_async_copy(e_ref.at[side], out_hbm.at[to, 9], sems.at[side, 7])

    for copy in arrivals(0):
        copy.start()
    rank_ids = lax.broadcasted_iota(jnp.int32, (HALF, 512), 0)
    band_ref[0, 0] = jnp.zeros((HALF, 512), BF)
    band_ref[2, 2] = jnp.zeros((HALF, 512), BF)
    for j in range(3):
        if j < 2:
            for copy in arrivals(j + 1):
                copy.start()
        fill_weights(w_ref, x_ref.at[:, :, :, :, pl.ds(j * TILE, TILE)])
        for copy in arrivals(j):
            copy.wait()
        v = jnp.concatenate([b_ref[j, :, c].reshape(3 * HALF, TILE) for c in range(2)], axis=1)
        prod = jnp.dot(v, w_ref[...], preferred_element_type=F32)
        for n in range(3):
            i = place * 3 + j + n - 1
            rank = ranks_ref[j, jnp.clip(i, 0, last_row)]
            kept = jnp.where(rank_ids + HALF < rank, prod[n * HALF : (n + 1) * HALF], 0.0).astype(BF)
            il = j + n - 1
            if il < 0:
                e_ref[0] = kept
            elif il > 2:
                e_ref[1] = kept
            else:
                band_ref[il, 2 - n] = kept
        for h in range(4):
            rows = slice(h * 12, (h + 1) * 12)
            v = jnp.concatenate([v_ref[j, rows, c].reshape(12 * HALF, TILE) for c in range(2)], axis=1)
            prod = jnp.dot(v, w_ref[...], preferred_element_type=F32)
            for n in range(12):
                i = h * 12 + n
                kept = jnp.where(rank_ids < ranks_ref[j, i], prod[n * HALF : (n + 1) * HALF], 0.0)
                o_ref[j, i % 3, i // 3] = kept.astype(BF)
        for copy in sends(j):
            copy.start()

    @pl.when(place > 0)
    def _():
        edge(0).start()

    @pl.when(place < owners - 1)
    def _():
        edge(1).start()

    for j in range(3):
        for copy in sends(j):
            copy.wait()

    @pl.when(place > 0)
    def _():
        edge(0).wait()

    @pl.when(place < owners - 1)
    def _():
        edge(1).wait()


def coefficients(spectra, v_factors, ranks, place):
    rows, cols = v_factors.shape[:2]
    whole = pl.BlockSpec(memory_space=pltpu.VMEM)
    scalars = pl.BlockSpec(memory_space=pltpu.SMEM)
    return pl.pallas_call(
        coeff_kernel,
        in_specs=[scalars, scalars, whole, pl.BlockSpec(memory_space=pl.ANY)],
        out_specs=[pl.BlockSpec(memory_space=pl.ANY), whole],
        out_shape=[
            jax.ShapeDtypeStruct((rows // 3, 10, HALF, 512), BF),
            jax.ShapeDtypeStruct((3, 3, HALF, 512), BF),
        ],
        scratch_shapes=[
            pltpu.VMEM((cols, rows, 2, HALF, TILE), BF),
            pltpu.VMEM((cols, 3, 2, HALF, TILE), BF),
            pltpu.VMEM((cols, 3, rows // 3, HALF, 512), BF),
            pltpu.VMEM((2, HALF, 512), BF),
            pltpu.VMEM((512, 512), BF),
            pltpu.SemaphoreType.DMA((3, 8)),
        ],
        compiler_params=params(52),
        cost_estimate=pl.CostEstimate(
            flops=2 * rows * cols * HALF * 512 * 512, bytes_accessed=10 * 2**20, transcendentals=0
        ),
    )(place, ranks, spectra, v_factors)


def response_kernel(
    place_ref, c_ref, u_ref, u_hbm, band_ref, minus_hbm, plus_hbm, gram_ref, cb_ref, ub_ref, z_ref, sems
):
    all_cols = u_hbm.shape[1]
    owners = c_ref.shape[0]
    place = place_ref[0]

    def arrivals(i):
        cols = [jnp.clip(place * 3 + i + n - 1, 0, all_cols - 1) for n in range(3)]
        return [
            pltpu.make_async_copy(
                u_hbm.at[i, cols[n], :, pl.ds(HALF, HALF), :], ub_ref.at[i, n], sems.at[i, n]
            )
            for n in range(3)
        ]

    def sends(i):
        lanes = pl.ds(i * TILE, TILE)
        return [
            pltpu.make_async_copy(z_ref.at[i, n], ref.at[0, :, :, lanes], sems.at[i, 3 + n])
            for n, ref in enumerate((minus_hbm, plus_hbm))
        ]

    def product(left, right):
        depth = left.shape[0] * HALF
        right = jnp.concatenate([right[:, c].reshape(depth, TILE) for c in range(2)], axis=1)
        left = left.reshape(depth, 512)
        return lax.dot_general(left, right, (((0,), (0,)), ((), ())), preferred_element_type=F32)

    for i in range(3):
        for copy in arrivals(i):
            copy.start()
    below = c_ref[jnp.maximum(place - 1, 0), 9]
    above = c_ref[jnp.minimum(place + 1, owners - 1), 9]
    for i in range(3):
        for n in range(3):
            cb_ref[i, n] = band_ref[i, n]
        cb_ref[i, 3] = jnp.zeros((HALF, 512), BF)
        ub_ref[i, 3] = jnp.zeros((2, HALF, TILE), BF)
    cb_ref[0, 0] = jnp.where(place > 0, below, jnp.zeros((), BF))
    cb_ref[2, 2] = jnp.where(place < owners - 1, above, jnp.zeros((), BF))
    def settle(i, prod):
        prod += product(cb_ref[i], ub_ref[i])
        re = (prod[:256, :256] - prod[256:, 256:]).astype(BF)
        im = prod[256:, :256] + prod[:256, 256:]
        im = jnp.concatenate([im[:128], -im[128:]], axis=0).astype(BF)
        z_ref[i, 0, 0] = re[:128]
        z_ref[i, 0, 1] = im[:128]
        z_ref[i, 1, 0] = re[128:]
        z_ref[i, 1, 1] = im[128:]

    last = None
    for i in range(3):
        prod = product(c_ref[:, 3 * i : 3 * i + 3].reshape(3 * owners, HALF, 512), u_ref[i])
        if i == 0:
            for n in range(3):
                for copy in arrivals(n):
                    copy.wait()
        else:
            settle(i - 1, last)
            for copy in sends(i - 1):
                copy.start()
        last = prod
    settle(2, last)
    for copy in sends(2):
        copy.start()
    rows = [jnp.concatenate([z_ref[i, m, c] for i in range(3)], axis=1) for c in range(2) for m in range(2)]
    gram = lax.dot_general(
        jnp.concatenate(rows, axis=0),
        jnp.concatenate([rows[1], rows[3]], axis=0),
        (((1,), (1,)), ((), ())),
        preferred_element_type=F32,
    )
    parts = (gram[:256, :128] + gram[256:, 128:], gram[256:, :128] - gram[:256, 128:])
    for m, scale in enumerate((1.0 / math.sqrt(R), 1.0 / R)):
        for c, part in enumerate(parts):
            gram_ref[:, m, c] = (part[m * 128 : (m + 1) * 128] * scale).reshape(16, 8, 128)
    for i in range(3):
        for copy in sends(i):
            copy.wait()


def respond(coeffs, u_held, u_factors, band, place):
    rows, all_cols = u_factors.shape[:2]
    whole = pl.BlockSpec(memory_space=pltpu.VMEM)
    anywhere = pl.BlockSpec(memory_space=pl.ANY)
    return pl.pallas_call(
        response_kernel,
        in_specs=[pl.BlockSpec(memory_space=pltpu.SMEM), whole, whole, anywhere, whole],
        out_specs=[anywhere, anywhere, whole],
        scratch_shapes=[
            pltpu.VMEM((rows, 4, HALF, 512), BF),
            pltpu.VMEM((rows, 4, 2, HALF, TILE), BF),
            pltpu.VMEM((rows, 2, 2, 128, TILE), BF),
            pltpu.SemaphoreType.DMA((3, 5)),
        ],
        out_shape=[
            jax.ShapeDtypeStruct((1, 2, 128, rows * TILE), BF),
            jax.ShapeDtypeStruct((1, 2, 128, rows * TILE), BF),
            jax.ShapeDtypeStruct((16, 2, 2, 8, 128), F32),
        ],
        compiler_params=params(40),
        cost_estimate=pl.CostEstimate(
            flops=2 * 144 * HALF * 512 * 512, bytes_accessed=11 * 2**20, transcendentals=0
        ),
    )(place, coeffs, u_held, u_factors, band)


def on_device(plus_time, minus_time, gate_starts, tile_ranks, u_factors, v_factors):
    u_factors, v_factors, ranks = u_factors[0], v_factors[0], tile_ranks[0].T
    place = lax.axis_index(TILES).astype(jnp.int32).reshape(1)
    local_spec = dft(plus_time, minus_time, gate_starts.T, make_table(8, 128).astype(F32))
    spectra = lax.all_to_all(local_spec, FREQ, 0, 0, tiled=True)
    spectra, u_held = lax.optimization_barrier((spectra, held(u_factors)))
    coeffs, band = coefficients(spectra, v_factors, ranks, place)
    arrived = lax.all_to_all(coeffs, TILES, 0, 0, tiled=True)
    minus_new, plus_new, gram = respond(arrived, u_held, u_factors, band, place)
    sums = lax.all_to_all(gram, TILES, 0, 0, tiled=True).sum(axis=0)
    return (minus_new, plus_new, sums[None, 0], sums[None, 1])


def solution(mesh):
    torus = Mesh(mesh.devices.reshape(4, 2, 4, 4), (*FREQ, *TILES))
    in_specs = (
        P(FREQ, None, TILES),
        P(FREQ, None, TILES),
        P(FREQ, TILES),
        P(FREQ, None, TILES),
        P(FREQ, TILES, None, None, None, None),
        P(FREQ, None, TILES, None, None, None),
    )
    out_specs = (
        P(FREQ, None, None, TILES),
        P(FREQ, None, None, TILES),
        P(FREQ, None, TILES, None),
        P(FREQ, None, TILES, None),
    )
    return jax.shard_map(
        on_device, mesh=torus, in_specs=in_specs, out_specs=out_specs, check_vma=False
    )
```

```python
import functools
import math

import jax
import jax.numpy as jnp
from jax import lax
from jax.experimental import pallas as pl
from jax.experimental.pallas import tpu as pltpu
from jax.sharding import Mesh
from jax.sharding import PartitionSpec as P

R = 12288
GATE = 64
TILE = 256
HALF = 32
FREQ = ("fx", "fc")
TILES = ("ty", "tz")
BF = jnp.bfloat16
F32 = jnp.float32


def make_table(freq_count, sample_count):
    row_ids = lax.broadcasted_iota(jnp.int32, (2 * freq_count, sample_count), 0)
    sample_ids = lax.broadcasted_iota(jnp.int32, (2 * freq_count, sample_count), 1)
    phase_ids = row_ids // 2 * sample_ids % sample_count
    angles = phase_ids.astype(F32) * (2.0 * math.pi / sample_count)
    amplitude = 1.0 / math.sqrt(GATE)
    return jnp.where(
        row_ids % 2 == 0, jnp.cos(angles) * amplitude, -jnp.sin(angles) * amplitude
    ).astype(BF)


def params(mib=56):
    return pltpu.CompilerParams(vmem_limit_bytes=mib * 2**20)


def dft_kernel(starts_ref, tab_ref, plus_ref, minus_ref, out_ref, rows_ref, t_ref):
    b = pl.program_id(0)

    @pl.when(b == 0)
    def _():
        rows = jnp.broadcast_to(tab_ref[...][:, None], (16, 16, 128)).reshape(256, 128)
        rows_ref[:, :128] = rows
        rows_ref[:, 128:] = rows

    lane = lax.broadcasted_iota(jnp.int32, (1, 256), 1)
    sample = lane & 127
    upper = lane >= 128
    row_source = lax.broadcasted_iota(jnp.int32, (256, 256), 0) & 15
    for p in range(8):
        start = jnp.where(upper, starts_ref[b, 2 * p + 1], starts_ref[b, 2 * p])
        inside = (sample >= start) & (sample < start + GATE)
        source = jnp.where(inside, jnp.where(upper, 2 * p + 1, 2 * p), -1)
        table = jnp.where(row_source == source, rows_ref[...], 0.0).astype(BF)
        t_ref[:, p * 256 : (p + 1) * 256] = table
    for q, ref in enumerate((plus_ref, minus_ref)):
        prod = jnp.dot(t_ref[...], ref[...].reshape(2048, 256), preferred_element_type=F32)
        prod = prod.reshape(8, 2, 16, 256)
        out_ref[:, 0, q] = prod[:, 0].astype(BF)
        out_ref[:, 1, q] = (prod[:, 1] if q == 0 else -prod[:, 1]).astype(BF)


def dft(plus_time, minus_time, gate_starts, table):
    sources, samples, receivers = plus_time.shape
    blocks = receivers // TILE
    data = pl.BlockSpec((sources, samples, TILE), lambda b: (0, 0, b))
    return pl.pallas_call(
        dft_kernel,
        grid=(blocks,),
        in_specs=[
            pl.BlockSpec(memory_space=pltpu.SMEM),
            pl.BlockSpec((16, 128), lambda b: (0, 0)),
            data,
            data,
        ],
        out_specs=pl.BlockSpec((8, 2, 2, 16, TILE), lambda b: (0, 0, 0, 0, b)),
        out_shape=jax.ShapeDtypeStruct((8, 2, 2, 16, receivers), BF),
        scratch_shapes=[pltpu.VMEM((256, 256), F32), pltpu.VMEM((256, 2048), BF)],
        compiler_params=params(),
        cost_estimate=pl.CostEstimate(
            flops=2 * 2 * 256 * 2048 * receivers, bytes_accessed=7 * 2**20, transcendentals=0
        ),
    )(gate_starts, table, plus_time, minus_time)


def hold_kernel(u_hbm, v_hbm, u_ref, v_ref, sems):
    low = pl.ds(0, HALF)
    copies = [
        pltpu.make_async_copy(v_hbm.at[:, :, :, low, :], v_ref, sems.at[0]),
        pltpu.make_async_copy(u_hbm.at[:, :, :, low, :], u_ref, sems.at[1]),
    ]
    for copy in copies:
        copy.start()
    for copy in copies:
        copy.wait()


def held(u_factors, v_factors):
    anywhere = pl.BlockSpec(memory_space=pl.ANY)
    whole = pl.BlockSpec(memory_space=pltpu.VMEM)
    shapes = [(*f.shape[:3], HALF, TILE) for f in (u_factors, v_factors)]
    return pl.pallas_call(
        hold_kernel,
        in_specs=[anywhere, anywhere],
        out_specs=[whole, whole],
        out_shape=[jax.ShapeDtypeStruct(shape, BF) for shape in shapes],
        scratch_shapes=[pltpu.SemaphoreType.DMA((2,))],
        compiler_params=params(44),
        cost_estimate=pl.CostEstimate(flops=0, bytes_accessed=10 * 2**20, transcendentals=0),
    )(u_factors, v_factors)


def fill_weights(w_ref, x_ref):
    for q in range(2):
        re = x_ref[:, 0, q].reshape(128, TILE).T
        im = x_ref[:, 1, q].reshape(128, TILE).T
        near, far = slice(q * 128, (q + 1) * 128), slice(256 + q * 128, 384 + q * 128)
        w_ref[0:256, near] = re
        w_ref[0:256, far] = im
        w_ref[256:512, near] = -im
        w_ref[256:512, far] = re


def coeff_kernel(
    place_ref, ranks_ref, x_ref, v_ref, v_hbm, out_hbm, band_ref, b_ref, o_ref, e_ref, w_ref, sems
):
    last_row = v_hbm.shape[0] - 1
    owners = out_hbm.shape[0]
    place = place_ref[0]

    def arrivals(j):
        copies = []
        for n in range(3):
            i = jnp.clip(place * 3 + j + n - 1, 0, last_row)
            src = v_hbm.at[i, j, :, pl.ds(HALF, HALF), :]
            copies.append(pltpu.make_async_copy(src, b_ref.at[j, n], sems.at[j, 1 + n]))
        return copies

    def sends(j):
        return [
            pltpu.make_async_copy(o_ref.at[j, i], out_hbm.at[:, 3 * i + j], sems.at[j, 4 + i])
            for i in range(3)
        ]

    def edge(side):
        to = jnp.clip(place + 2 * side - 1, 0, owners - 1)
        return pltpu.make_async_copy(e_ref.at[side], out_hbm.at[to, 9], sems.at[side, 7])

    for copy in arrivals(0):
        copy.start()
    rank_ids = lax.broadcasted_iota(jnp.int32, (HALF, 512), 0)
    band_ref[0, 0] = jnp.zeros((HALF, 512), BF)
    band_ref[2, 2] = jnp.zeros((HALF, 512), BF)
    for j in range(3):
        if j < 2:
            for copy in arrivals(j + 1):
                copy.start()
        fill_weights(w_ref, x_ref.at[:, :, :, :, pl.ds(j * TILE, TILE)])
        for copy in arrivals(j):
            copy.wait()
        v = jnp.concatenate([b_ref[j, :, c].reshape(3 * HALF, TILE) for c in range(2)], axis=1)
        prod = jnp.dot(v, w_ref[...], preferred_element_type=F32)
        for n in range(3):
            i = place * 3 + j + n - 1
            rank = ranks_ref[j, jnp.clip(i, 0, last_row)]
            kept = jnp.where(rank_ids + HALF < rank, prod[n * HALF : (n + 1) * HALF], 0.0).astype(BF)
            il = j + n - 1
            if il < 0:
                e_ref[0] = kept
            elif il > 2:
                e_ref[1] = kept
            else:
                band_ref[il, 2 - n] = kept
        for h in range(4):
            rows = slice(h * 12, (h + 1) * 12)
            v = jnp.concatenate([v_ref[rows, j, c].reshape(12 * HALF, TILE) for c in range(2)], axis=1)
            prod = jnp.dot(v, w_ref[...], preferred_element_type=F32)
            for n in range(12):
                i = h * 12 + n
                kept = jnp.where(rank_ids < ranks_ref[j, i], prod[n * HALF : (n + 1) * HALF], 0.0)
                o_ref[j, i % 3, i // 3] = kept.astype(BF)
        for copy in sends(j):
            copy.start()

    @pl.when(place > 0)
    def _():
        edge(0).start()

    @pl.when(place < owners - 1)
    def _():
        edge(1).start()

    for j in range(3):
        for copy in sends(j):
            copy.wait()

    @pl.when(place > 0)
    def _():
        edge(0).wait()

    @pl.when(place < owners - 1)
    def _():
        edge(1).wait()


def coefficients(spectra, v_held, v_factors, ranks, place):
    rows, cols = v_factors.shape[:2]
    whole = pl.BlockSpec(memory_space=pltpu.VMEM)
    scalars = pl.BlockSpec(memory_space=pltpu.SMEM)
    return pl.pallas_call(
        coeff_kernel,
        in_specs=[scalars, scalars, whole, whole, pl.BlockSpec(memory_space=pl.ANY)],
        out_specs=[pl.BlockSpec(memory_space=pl.ANY), whole],
        out_shape=[
            jax.ShapeDtypeStruct((rows // 3, 10, HALF, 512), BF),
            jax.ShapeDtypeStruct((3, 3, HALF, 512), BF),
        ],
        scratch_shapes=[
            pltpu.VMEM((cols, 3, 2, HALF, TILE), BF),
            pltpu.VMEM((cols, 3, rows // 3, HALF, 512), BF),
            pltpu.VMEM((2, HALF, 512), BF),
            pltpu.VMEM((512, 512), BF),
            pltpu.SemaphoreType.DMA((3, 8)),
        ],
        compiler_params=params(40),
        cost_estimate=pl.CostEstimate(
            flops=2 * rows * cols * HALF * 512 * 512, bytes_accessed=10 * 2**20, transcendentals=0
        ),
    )(place, ranks, spectra, v_held, v_factors)


def response_kernel(
    place_ref, c_ref, u_ref, u_hbm, band_ref, minus_hbm, plus_hbm, gram_ref, cb_ref, ub_ref, z_ref, sems
):
    all_cols = u_hbm.shape[1]
    owners = c_ref.shape[0]
    place = place_ref[0]

    def arrivals(i):
        cols = [jnp.clip(place * 3 + i + n - 1, 0, all_cols - 1) for n in range(3)]
        return [
            pltpu.make_async_copy(
                u_hbm.at[i, cols[n], :, pl.ds(HALF, HALF), :], ub_ref.at[i, n], sems.at[i, n]
            )
            for n in range(3)
        ]

    def sends(i):
        lanes = pl.ds(i * TILE, TILE)
        return [
            pltpu.make_async_copy(z_ref.at[i, n], ref.at[0, :, :, lanes], sems.at[i, 3 + n])
            for n, ref in enumerate((minus_hbm, plus_hbm))
        ]

    def product(left, right):
        depth = left.shape[0] * HALF
        right = jnp.concatenate([right[:, c].reshape(depth, TILE) for c in range(2)], axis=1)
        left = left.reshape(depth, 512)
        return lax.dot_general(left, right, (((0,), (0,)), ((), ())), preferred_element_type=F32)

    for i in range(3):
        for copy in arrivals(i):
            copy.start()
    below = c_ref[jnp.maximum(place - 1, 0), 9]
    above = c_ref[jnp.minimum(place + 1, owners - 1), 9]
    for i in range(3):
        for n in range(3):
            cb_ref[i, n] = band_ref[i, n]
        cb_ref[i, 3] = jnp.zeros((HALF, 512), BF)
        ub_ref[i, 3] = jnp.zeros((2, HALF, TILE), BF)
    cb_ref[0, 0] = jnp.where(place > 0, below, jnp.zeros((), BF))
    cb_ref[2, 2] = jnp.where(place < owners - 1, above, jnp.zeros((), BF))
    def settle(i, prod):
        prod += product(cb_ref[i], ub_ref[i])
        re = (prod[:256, :256] - prod[256:, 256:]).astype(BF)
        im = prod[256:, :256] + prod[:256, 256:]
        im = jnp.concatenate([im[:128], -im[128:]], axis=0).astype(BF)
        z_ref[i, 0, 0] = re[:128]
        z_ref[i, 0, 1] = im[:128]
        z_ref[i, 1, 0] = re[128:]
        z_ref[i, 1, 1] = im[128:]

    last = None
    for i in range(3):
        prod = product(c_ref[:, 3 * i : 3 * i + 3].reshape(3 * owners, HALF, 512), u_ref[i])
        if i == 0:
            for n in range(3):
                for copy in arrivals(n):
                    copy.wait()
        else:
            settle(i - 1, last)
            for copy in sends(i - 1):
                copy.start()
        last = prod
    settle(2, last)
    for copy in sends(2):
        copy.start()
    rows = [jnp.concatenate([z_ref[i, m, c] for i in range(3)], axis=1) for c in range(2) for m in range(2)]
    gram = lax.dot_general(
        jnp.concatenate(rows, axis=0),
        jnp.concatenate([rows[1], rows[3]], axis=0),
        (((1,), (1,)), ((), ())),
        preferred_element_type=F32,
    )
    parts = (gram[:256, :128] + gram[256:, 128:], gram[256:, :128] - gram[:256, 128:])
    for m, scale in enumerate((1.0 / math.sqrt(R), 1.0 / R)):
        for c, part in enumerate(parts):
            gram_ref[:, m, c] = (part[m * 128 : (m + 1) * 128] * scale).reshape(16, 8, 128)
    for i in range(3):
        for copy in sends(i):
            copy.wait()


def respond(coeffs, u_held, u_factors, band, place):
    rows, all_cols = u_factors.shape[:2]
    whole = pl.BlockSpec(memory_space=pltpu.VMEM)
    anywhere = pl.BlockSpec(memory_space=pl.ANY)
    return pl.pallas_call(
        response_kernel,
        in_specs=[pl.BlockSpec(memory_space=pltpu.SMEM), whole, whole, anywhere, whole],
        out_specs=[anywhere, anywhere, whole],
        scratch_shapes=[
            pltpu.VMEM((rows, 4, HALF, 512), BF),
            pltpu.VMEM((rows, 4, 2, HALF, TILE), BF),
            pltpu.VMEM((rows, 2, 2, 128, TILE), BF),
            pltpu.SemaphoreType.DMA((3, 5)),
        ],
        out_shape=[
            jax.ShapeDtypeStruct((1, 2, 128, rows * TILE), BF),
            jax.ShapeDtypeStruct((1, 2, 128, rows * TILE), BF),
            jax.ShapeDtypeStruct((16, 2, 2, 8, 128), F32),
        ],
        compiler_params=params(40),
        cost_estimate=pl.CostEstimate(
            flops=2 * 144 * HALF * 512 * 512, bytes_accessed=11 * 2**20, transcendentals=0
        ),
    )(place, coeffs, u_held, u_factors, band)


def on_device(plus_time, minus_time, gate_starts, tile_ranks, u_factors, v_factors):
    u_factors, v_factors, ranks = u_factors[0], v_factors[0], tile_ranks[0].T
    place = lax.axis_index(TILES).astype(jnp.int32).reshape(1)
    local_spec = dft(plus_time, minus_time, gate_starts.T, make_table(8, 128).astype(F32))
    spectra = lax.all_to_all(local_spec, FREQ, 0, 0, tiled=True)
    u_held, v_held = held(u_factors, v_factors)
    spectra, u_held = lax.optimization_barrier((spectra, u_held))
    coeffs, band = coefficients(spectra, v_held, v_factors, ranks, place)
    arrived = lax.all_to_all(coeffs, TILES, 0, 0, tiled=True)
    minus_new, plus_new, gram = respond(arrived, u_held, u_factors, band, place)
    sums = lax.all_to_all(gram, TILES, 0, 0, tiled=True).sum(axis=0)
    return (minus_new, plus_new, sums[None, 0], sums[None, 1])


def solution(mesh):
    torus = Mesh(mesh.devices.reshape(4, 2, 4, 4), (*FREQ, *TILES))
    in_specs = (
        P(FREQ, None, TILES),
        P(FREQ, None, TILES),
        P(FREQ, TILES),
        P(FREQ, None, TILES),
        P(FREQ, TILES, None, None, None, None),
        P(FREQ, None, TILES, None, None, None),
    )
    out_specs = (
        P(FREQ, None, None, TILES),
        P(FREQ, None, None, TILES),
        P(FREQ, None, TILES, None),
        P(FREQ, None, TILES, None),
    )
    return jax.shard_map(
        on_device, mesh=torus, in_specs=in_specs, out_specs=out_specs, check_vma=False
    )
```
